256 devices in a mesh: section: 8 (over x_hi, y), seq: 32 (over z, x_lo, core).
Axes of the slice: x: 4 (x_hi: 2, x_lo: 2; x = x_hi * 2 + x_lo), y: 4, z: 8, core: 2. Of those that a mesh axis runs over, the one named last changes fastest.
Arguments:
- queries: bfloat16 [8, 256, 2688], P('section'), may hold values from -10 to 10
- keys: bfloat16 [8, 4096, 2688], P('section', 'seq'), may hold values from -10 to 10
- values: bfloat16 [8, 4096, 2688], P('section', 'seq'), may hold values from -6 to 6
- out_grad: bfloat16 [8, 256, 5280], P('section'), may hold values from -6 to 6
- w_out: bfloat16 [2688, 5280], P('seq'), may hold values from -0.125 to 0.125
- window_start: int32 [256], replicated, may hold values from 0 to 4095, as said below
Outputs:
- grad_queries: bfloat16 [8, 2688, 256], P('section', 'seq')
- grad_keys: bfloat16 [8, 4096, 2688], P('section', 'seq')
- grad_values: bfloat16 [8, 4096, 2688], P('section', 'seq')
- grad_w_out: bfloat16 [2688, 5280], P('seq', 'section')
The draws below stay inside these ranges and needn't reach their ends.
Inputs may be any that keep to these rules, and one draw needn't show every extreme that they name: window_start[i] lies between 0 and the query's own position 3840 + i and never falls as i grows.
All inputs are finite; a program needn't handle non-finite values.
Results may differ from the reference program's by a relative error of at most 0.0088.
Values may be sent and summed in bfloat16 or wider, within the bound.
No kernel may reach another device: no remote copies, remote signals or barrier semaphores. Data moves between devices by JAX's collectives and lax.ppermute only.
A program may use at most 64 MiB of HBM per device.

```python
import jax
import jax.numpy as jnp
from jax import lax

D = 5280
HEADS = 28
HEAD_DIM = 96
QB = 256
KV_DEV = 128
ITERS = 8
CONTEXT = 4096
N_SEQ = 32


def draw_queries(key, part):
    key = jax.random.fold_in(key, 11)
    first = jax.random.fold_in(key, 0)
    shape = (ITERS, QB, HEADS * HEAD_DIM)
    drawn = jnp.clip(1.6 * jax.random.normal(first, shape, jnp.float32), -9.6, 9.6)
    return drawn.astype(jnp.bfloat16)


def draw_keys(key, part):
    key = jax.random.fold_in(key, 23)
    first = jax.random.fold_in(key, 0)
    shape = (ITERS, CONTEXT, HEADS * HEAD_DIM)
    drawn = jnp.clip(1.6 * jax.random.normal(first, shape, jnp.float32), -9.6, 9.6)
    return drawn.astype(jnp.bfloat16)


def draw_window_start(key, part):
    key = jax.random.fold_in(key, 37)
    first, second, third = jax.random.split(key, 3)
    far_start = jax.random.randint(first, (), 0, CONTEXT // 8 + 1)
    first_break = jax.random.randint(second, (), QB // 2, 3 * QB // 4)
    second_break = jax.random.randint(third, (), 3 * QB // 4 + 1, QB)
    rows = jnp.arange(QB, dtype=jnp.int32)
    offset = CONTEXT - QB
    starts = jnp.where(rows < first_break, far_start, jnp.where(rows < second_break, offset + first_break, offset + second_break))
    starts = jnp.where(rows == 0, 0, starts)
    starts = jnp.where(rows == QB - 1, CONTEXT - 1, starts)
    return starts.astype(jnp.int32)


def steps_of(stream_key, extent, pieces, low, largest):
    loudness, own = 1.0, jax.random.fold_in(stream_key, 6)
    for axis_at, blocks in pieces:
        steps = jnp.exp(jax.random.uniform(jax.random.fold_in(own, axis_at), (blocks,), jnp.float32, low / len(pieces), largest / len(pieces)))
        loudness = loudness * jnp.repeat(steps, extent[axis_at] // blocks).reshape([-1 if axis == axis_at else 1 for axis in range(len(extent))])
    return loudness


def gaussian(stream_key, dims, deviation, most, cuts=(), kind=jnp.bfloat16):
    result = jax.random.normal(stream_key, dims, jnp.float32) * deviation
    if len(cuts) > 0:
        result = steps_of(stream_key, dims, cuts, -0.22, 0.18) * result
    return jnp.clip(result, min=-most, max=most).astype(kind)


def setup_inputs(seed: int = 0) -> dict:
    seeds = jax.random.split(jax.random.key(seed), 7)
    return {
        "queries": draw_queries(jax.random.fold_in(seeds[6], 71), 0),
        "keys": draw_keys(jax.random.fold_in(seeds[6], 71), 0),
        "values": gaussian(seeds[2], (ITERS, KV_DEV * N_SEQ, HEADS * HEAD_DIM), 1.0, 6.0, ((0, 8), (1, 32))),
        "out_grad": gaussian(seeds[3], (ITERS, QB, D), 1.0, 6.0, ((0, 8),)),
        "w_out": gaussian(seeds[4], (HEADS * HEAD_DIM, D), (HEADS * HEAD_DIM) ** -0.5, 0.125, ((0, 32),)),
        "window_start": draw_window_start(jax.random.fold_in(seeds[6], 71), 0),
    }


NEG = -1e30


def reference(queries, keys, values, out_grad, w_out, window_start):
    scale = HEAD_DIM ** -0.5
    width = HEADS * HEAD_DIM
    key_pos = jnp.arange(CONTEXT, dtype=jnp.int32)
    query_pos = CONTEXT - QB + jnp.arange(QB, dtype=jnp.int32)
    visible = (key_pos[None, :] >= window_start[:, None]) & (key_pos[None, :] <= query_pos[:, None])

    def step(carry, item):
        query, key_rows, value_rows, cotangent = item
        qh = query.astype(jnp.float32).reshape(QB, HEADS, HEAD_DIM)
        kh = key_rows.astype(jnp.float32).reshape(CONTEXT, HEADS, HEAD_DIM)
        vh = value_rows.astype(jnp.float32).reshape(CONTEXT, HEADS, HEAD_DIM)
        scores = jnp.einsum('qhd,khd->hqk', qh, kh) * scale
        scores = jnp.where(visible[None], scores, NEG)
        top = jnp.max(scores, axis=2)
        expo = jnp.exp(scores - top[..., None])
        probs = expo / jnp.sum(expo, axis=2)[..., None]
        probs_b = lax.optimization_barrier(probs.astype(jnp.bfloat16)).astype(jnp.float32)
        attended = jnp.einsum('hqk,khd->qhd', probs_b, vh).reshape(QB, width).astype(jnp.bfloat16)
        d_att = jnp.dot(cotangent, w_out.T, preferred_element_type=jnp.float32).astype(jnp.bfloat16)
        carry = carry + jnp.dot(attended.T, cotangent, preferred_element_type=jnp.float32)
        att_f = lax.optimization_barrier(attended).astype(jnp.float32).reshape(QB, HEADS, HEAD_DIM)
        dah = lax.optimization_barrier(d_att).astype(jnp.float32).reshape(QB, HEADS, HEAD_DIM)
        dots = jnp.sum(att_f * dah, axis=2).T
        dprobs = jnp.einsum('qhd,khd->hqk', dah, vh)
        dscores = probs * (dprobs - dots[..., None])
        dscores_b = lax.optimization_barrier(dscores.astype(jnp.bfloat16)).astype(jnp.float32)
        grad_v = jnp.einsum('hqk,qhd->khd', probs_b, dah).reshape(CONTEXT, width).astype(jnp.bfloat16)
        grad_k = (scale * jnp.einsum('hqk,qhd->khd', dscores_b, qh)).reshape(CONTEXT, width).astype(jnp.bfloat16)
        grad_q = (scale * jnp.einsum('hqk,khd->hdq', dscores_b, kh)).reshape(width, QB).astype(jnp.bfloat16)
        return carry, (grad_q, grad_k, grad_v)

    start = jnp.zeros((width, D), jnp.float32)
    summed, (grad_q, grad_k, grad_v) = lax.scan(step, start, (queries, keys, values, out_grad))
    return grad_q, grad_k, grad_v, summed.astype(jnp.bfloat16)
```

```python
import functools

import jax
import jax.numpy as jnp
from jax import lax
from jax.experimental import pallas as pl
from jax.experimental.pallas import tpu as pltpu
from jax.sharding import Mesh, PartitionSpec as P

HEADS = 28
HEAD_DIM = 96
GROUPS = 4
GROUP_HEADS = HEADS // GROUPS
GROUP_WIDTH = GROUP_HEADS * HEAD_DIM
BLOCK = 8
NEG = -(2.0**99)
SCALE = HEAD_DIM ** (-0.5)
BLOCK_AXES = ("zl", "x_lo", "core")
SEQ_AXES = ("zp",) + BLOCK_AXES
F32 = jnp.float32
BF16 = jnp.bfloat16
VMEM_LIMIT = 48 * 1024 * 1024
NT = (((1,), (1,)), ((), ()))
NN = (((1,), (0,)), ((), ()))
TN = (((0,), (0,)), ((), ()))


def mm(a, b, dims):
    return lax.dot_general(a, b, dims, preferred_element_type=F32)


def pack_kernel(place, k_ref, v_ref, q_ref, *outs):
    zp = place[0]
    kv_len = k_ref.shape[0]
    for g in range(GROUPS):
        cols = slice(g * GROUP_WIDTH, (g + 1) * GROUP_WIDTH)
        for s in range(GROUPS):

            @pl.when(lax.rem(zp + s, GROUPS) == g)
            def _():
                outs[s][:kv_len, :] = k_ref[:, cols]
                outs[s][kv_len:, :] = v_ref[:, cols]
                if s == 0:
                    outs[GROUPS][...] = q_ref[:, cols]


def unpack_kernel(place, s0, s1, s2, s3, gk_ref, gv_ref):
    zp = place[0]
    kv_len = gk_ref.shape[0]
    slots = (s0, s1, s2, s3)
    for g in range(GROUPS):
        cols = slice(g * GROUP_WIDTH, (g + 1) * GROUP_WIDTH)
        for s in range(GROUPS):

            @pl.when(lax.rem(zp + s, GROUPS) == g)
            def _():
                gk_ref[:, cols] = slots[s][:kv_len, :]
                gv_ref[:, cols] = slots[s][kv_len:, :]


def set_up(place, ws_ref, d_ref, bias, d_all):
    zp, member = place[0], place[1]
    q_len = ws_ref.shape[1]
    kv_len = bias.shape[0] // GROUPS
    context = kv_len * GROUPS * BLOCK
    rows = lax.broadcasted_iota(jnp.int32, (kv_len, q_len), 0)
    query_pos = context - q_len + lax.broadcasted_iota(jnp.int32, (kv_len, q_len), 1)
    for s in range(GROUPS):
        owner = lax.rem(zp + GROUPS - s, GROUPS) * BLOCK + member
        key_pos = owner * kv_len + rows
        visible = (key_pos >= ws_ref[...]) & (key_pos <= query_pos)
        bias[s * kv_len : (s + 1) * kv_len, :] = jnp.where(visible, 0.0, NEG)
    rows_each = d_ref.shape[1]
    for k in range(BLOCK):
        d_all[k * rows_each : (k + 1) * rows_each, :] = d_ref[k].astype(F32)


def head_cols(slots, lo, hi, cols):
    return jnp.concatenate([s[lo:hi, cols] for s in slots], axis=0)


def forward_kernel(place, ws_ref, q_ref, s0, s1, s2, s3, d_ref, out_ref, bias, d_all, att, payload):
    kv_len = s0.shape[0] // 2
    slots = (s0, s1, s2, s3)
    rows_each = d_ref.shape[1]
    set_up(place, ws_ref, d_ref, bias, d_all)
    payload[...] = jnp.zeros_like(payload)
    for h in range(GROUP_HEADS):
        cols = slice(h * HEAD_DIM, (h + 1) * HEAD_DIM)
        kh = head_cols(slots, 0, kv_len, cols)
        vh = head_cols(slots, kv_len, 2 * kv_len, cols)
        dh = d_all[cols, :].astype(BF16)
        scores = mm(kh, q_ref[:, cols], NT) * SCALE + bias[...]
        top = jnp.floor(jnp.max(scores, axis=0, keepdims=True) * 0.125) * 8.0
        expo = jnp.exp(scores - top)
        total = jnp.sum(expo, axis=0, keepdims=True)
        att[cols, :] = mm(vh, expo.astype(BF16), TN)
        dots = jnp.sum(expo * mm(vh, dh, NN), axis=0, keepdims=True)
        total_hi = total.astype(BF16).astype(F32)
        dots_hi = dots.astype(BF16).astype(F32)
        for n, row in enumerate((top, total_hi, total - total_hi, dots_hi, dots - dots_hi)):
            payload[0, 88 + 8 * n + h : 89 + 8 * n + h, :] = row
    for k in range(BLOCK):
        if k > 0:
            payload[k, 88:, :] = payload[0, 88:, :]
        payload[k, :rows_each, :] = att[k * rows_each : (k + 1) * rows_each, :]
    out_ref[...] = payload[...].astype(BF16)


def backward_kernel(
    place, ws_ref, q_ref, s0, s1, s2, s3, d_ref, ex_ref, o0, o1, o2, o3, gq_ref, att_ref, bias, d_all, gq, stats, weights
):
    kv_len = s0.shape[0] // 2
    slots = (s0, s1, s2, s3)
    outs = (o0, o1, o2, o3)
    rows_each, q_len = att_ref.shape
    member = place[1]
    set_up(place, ws_ref, d_ref, bias, d_all)
    parts = [ex_ref[j].astype(F32) for j in range(BLOCK)]
    top = functools.reduce(jnp.maximum, [p[88:96] for p in parts])
    scaled = [jnp.exp(p[88:96] - top) for p in parts]
    total = sum(w * (p[96:104] + p[104:112]) for w, p in zip(scaled, parts))
    total = jnp.where(total > 0.0, total, 1.0)
    inverse = 1.0 / total
    dots = sum(w * (p[112:120] + p[120:128]) for w, p in zip(scaled, parts)) * inverse
    stats[0] = top
    stats[1] = inverse
    stats[2] = dots
    weights[...] = jnp.zeros_like(weights)
    row = lax.broadcasted_iota(jnp.int32, (rows_each, q_len), 0)
    first = row < (HEAD_DIM - rows_each) * member
    attended = jnp.zeros((rows_each, q_len), F32)
    for j in range(BLOCK):
        weights[j, 8:16, :] = scaled[j] * inverse
        before = weights[j, pl.ds(member + 7, 1), :]
        after = weights[j, pl.ds(member + 8, 1), :]
        attended += jnp.where(first, before, after) * parts[j][:rows_each]
    att_ref[...] = attended.astype(BF16)
    for h in range(GROUP_HEADS):
        cols = slice(h * HEAD_DIM, (h + 1) * HEAD_DIM)
        kh = head_cols(slots, 0, kv_len, cols)
        vh = head_cols(slots, kv_len, 2 * kv_len, cols)
        qh = q_ref[:, cols]
        dh = d_all[cols, :].astype(BF16)
        scores = mm(kh, qh, NT) * SCALE + bias[...]
        probs = jnp.exp(scores - stats[0, h : h + 1, :]) * stats[1, h : h + 1, :]
        dscores = probs * (mm(vh, dh, NN) - stats[2, h : h + 1, :])
        probs = probs.astype(BF16)
        dscores = dscores.astype(BF16)
        gk = (mm(dscores, qh, NN) * SCALE).astype(BF16)
        gv = mm(probs, dh, NT).astype(BF16)
        for s in range(GROUPS):
            part = slice(s * kv_len, (s + 1) * kv_len)
            outs[s][:kv_len, cols] = gk[part]
            outs[s][kv_len:, cols] = gv[part]
        gq[cols, :] = mm(kh, dscores, TN) * SCALE
    for k in range(BLOCK):
        gq_ref[k] = gq[k * rows_each : (k + 1) * rows_each, :].astype(BF16)


def weight_kernel(att_ref, cot_ref, out_ref, full):
    pieces, _, width = out_ref.shape
    full[...] = mm(att_ref[...], cot_ref[...], NN)
    for s in range(pieces):
        out_ref[s] = full[:, s * width : (s + 1) * width].astype(BF16)


SMEM = pl.BlockSpec(memory_space=pltpu.SMEM)
WHOLE = pl.BlockSpec(memory_space=pltpu.VMEM)


def call(kernel, n_in, out_shapes, scratch=(), scalars=1, flops=0, nbytes=0):
    return pl.pallas_call(
        kernel,
        out_shape=out_shapes,
        in_specs=[SMEM] * scalars + [WHOLE] * n_in,
        out_specs=jax.tree.map(lambda _: WHOLE, out_shapes),
        scratch_shapes=list(scratch),
        compiler_params=pltpu.CompilerParams(vmem_limit_bytes=VMEM_LIMIT),
        cost_estimate=pl.CostEstimate(flops=flops, bytes_accessed=nbytes, transcendentals=0),
    )


def shift(by):
    return [(i, (i + by) % GROUPS) for i in range(GROUPS)]


def local(queries, keys, values, out_grad, w_out, window_start):
    query, key_rows, value_rows, cotangent = queries[0], keys[0], values[0], out_grad[0]
    q_len = query.shape[0]
    kv_len = key_rows.shape[0]
    rows_each, model = w_out.shape
    sections = lax.axis_size("section")
    member = lax.axis_index(BLOCK_AXES)
    place = jnp.stack([lax.axis_index("zp"), member]).astype(jnp.int32)
    starts = window_start.reshape(1, q_len)
    sds = jax.ShapeDtypeStruct
    slot = sds((2 * kv_len, GROUP_WIDTH), BF16)

    *send, q_own = call(pack_kernel, 3, [slot] * GROUPS + [sds((q_len, GROUP_WIDTH), BF16)], nbytes=4_000_000)(
        place, key_rows, value_rows, query
    )
    slots = [send[0]] + [lax.ppermute(send[s], "zp", shift(s)) for s in range(1, GROUPS)]

    d_own = lax.dot_general(w_out, cotangent, NT, preferred_element_type=F32).astype(BF16)
    d_group = lax.all_to_all(jnp.broadcast_to(d_own[None], (BLOCK, rows_each, q_len)), BLOCK_AXES, 0, 0)

    positions = GROUPS * kv_len
    common = [pltpu.VMEM((positions, q_len), F32), pltpu.VMEM((GROUP_WIDTH, q_len), F32), pltpu.VMEM((GROUP_WIDTH, q_len), F32)]
    payload = call(
        forward_kernel,
        7,
        sds((BLOCK, 128, q_len), BF16),
        common + [pltpu.VMEM((BLOCK, 128, q_len), F32)],
        flops=2_000_000_000,
        nbytes=2_000_000,
    )(place, starts, q_own, *slots, d_group)
    exchanged = lax.all_to_all(payload, BLOCK_AXES, 0, 0)

    *back, gq_parts, attended = call(
        backward_kernel,
        8,
        [slot] * GROUPS + [sds((BLOCK, rows_each, q_len), BF16), sds((rows_each, q_len), BF16)],
        common + [pltpu.VMEM((3, 8, q_len), F32), pltpu.VMEM((BLOCK, 24, q_len), F32)],
        flops=3_000_000_000,
        nbytes=4_000_000,
    )(place, starts, q_own, *slots, d_group, exchanged)

    back = [back[0]] + [lax.ppermute(back[s], "zp", shift(-s)) for s in range(1, GROUPS)]

    gq = lax.all_to_all(gq_parts, BLOCK_AXES, 0, 0)
    grad_q = jnp.sum(gq.astype(F32), axis=0).astype(BF16)

    width = model // sections
    weight_parts = call(
        weight_kernel,
        2,
        sds((sections, rows_each, width), BF16),
        [pltpu.VMEM((rows_each, model), F32)],
        scalars=0,
        flops=2 * rows_each * q_len * model,
        nbytes=4_000_000,
    )(attended, cotangent)
    weight_parts = lax.all_to_all(weight_parts, "section", 0, 0)
    grad_weight = jnp.sum(weight_parts.astype(F32), axis=0).astype(BF16)

    grad_k, grad_v = call(unpack_kernel, 4, [sds((kv_len, HEADS * HEAD_DIM), BF16)] * 2, nbytes=3_000_000)(place, *back)
    return grad_q[None], grad_k[None], grad_v[None], grad_weight


def solution(mesh):
    sections = mesh.shape["section"]
    fine = Mesh(mesh.devices.reshape(sections, GROUPS, 2, 2, 2), ("section",) + SEQ_AXES)
    return jax.shard_map(
        local,
        mesh=fine,
        in_specs=(
            P("section", None, None),
            P("section", SEQ_AXES, None),
            P("section", SEQ_AXES, None),
            P("section", None, None),
            P(SEQ_AXES, None),
            P(),
        ),
        out_specs=(
            P("section", SEQ_AXES, None),
            P("section", SEQ_AXES, None),
            P("section", SEQ_AXES, None),
            P(SEQ_AXES, "section"),
        ),
        check_vma=False,
    )
```

```python
import functools

import jax
import jax.numpy as jnp
from jax import lax
from jax.experimental import pallas as pl
from jax.experimental.pallas import tpu as pltpu
from jax.sharding import Mesh, PartitionSpec as P

HEADS = 28
HEAD_DIM = 96
GROUPS = 4
GROUP_HEADS = HEADS // GROUPS
GROUP_WIDTH = GROUP_HEADS * HEAD_DIM
PIECES = 8
NEG = -(2.0**99)
SCALE = HEAD_DIM ** (-0.5)
SEQ_AXES = ("zp", "zl", "x_lo", "core")
F32 = jnp.float32
BF16 = jnp.bfloat16
VMEM_LIMIT = 48 * 1024 * 1024
COST = dict(
    pack=1, join=1, forward=2, core=1, attended=1, backward=3, weight=2, add=30, unpack=10, add4=1, sum=10
)
NT = (((1,), (1,)), ((), ()))
NN = (((1,), (0,)), ((), ()))
TN = (((0,), (0,)), ((), ()))


def mm(a, b, dims):
    return lax.dot_general(a, b, dims, preferred_element_type=F32)


def pack_kernel(place, k_ref, v_ref, q_ref, *outs):
    chip = place[0]
    for g in range(GROUPS):
        cols = slice(g * GROUP_WIDTH, (g + 1) * GROUP_WIDTH)
        for s in range(GROUPS):

            @pl.when(lax.bitwise_xor(chip, s) == g)
            def _():
                outs[s][0] = k_ref[:, cols]
                outs[s][1] = v_ref[:, cols]
                if s == 0:
                    outs[GROUPS][...] = q_ref[:, cols]


def unpack_kernel(place, s0, s1, s2, s3, gk_ref, gv_ref):
    chip = place[0]
    slots = (s0, s1, s2, s3)
    for g in range(GROUPS):
        cols = slice(g * GROUP_WIDTH, (g + 1) * GROUP_WIDTH)
        for s in range(GROUPS):

            @pl.when(lax.bitwise_xor(chip, s) == g)
            def _():
                gk_ref[:, cols] = slots[s][0]
                gv_ref[:, cols] = slots[s][1]


def set_mask(place, ws_ref, bias):
    chip, pair, core = place[0], place[1], place[2]
    q_len = ws_ref.shape[1]
    kv_len = bias.shape[0] // GROUPS
    context = kv_len * GROUPS * PIECES
    rows = lax.broadcasted_iota(jnp.int32, (kv_len, q_len), 0)
    query_pos = context - q_len + lax.broadcasted_iota(jnp.int32, (kv_len, q_len), 1)
    for s in range(GROUPS):
        owner = pair * PIECES + 2 * lax.bitwise_xor(chip, s) + core
        key_pos = owner * kv_len + rows
        visible = (key_pos >= ws_ref[...]) & (key_pos <= query_pos)
        bias[s * kv_len : (s + 1) * kv_len, :] = jnp.where(visible, 0.0, NEG)


def join_kernel(place, m0, m1, m2, m3, theirs_ref, out_ref, pieces, rows):
    pair, core = place[1], place[2]
    rows_each = m0.shape[0]
    for j, mine in enumerate((m0, m1, m2, m3)):
        at = 2 * lax.bitwise_xor(pair, j)
        pieces[at + core] = mine[...].astype(F32)
        pieces[at + 1 - core] = theirs_ref[j].astype(F32)
    for k in range(PIECES):
        rows[k * rows_each : (k + 1) * rows_each, :] = pieces[k]
    out_ref[...] = rows[...].astype(BF16)


def head(h):
    return slice(h * HEAD_DIM, (h + 1) * HEAD_DIM)


def joined(slots, which, cols):
    return jnp.concatenate([s[which, :, cols] for s in slots], axis=0)


def halve(place, full, pieces, keep_ref, send_ref):
    core = place[2]
    rows_each = keep_ref.shape[1]
    for k in range(PIECES):
        pieces[k] = full[k * rows_each : (k + 1) * rows_each, :]
    for b in range(GROUPS):
        keep_ref[b] = pieces[2 * b + core]
        send_ref[b] = pieces[2 * b + 1 - core].astype(BF16)


def forward_kernel(place, ws_ref, q_ref, s0, s1, s2, s3, d_ref, keep_ref, send_ref, stats_ref, bias, att, pieces):
    slots = (s0, s1, s2, s3)
    set_mask(place, ws_ref, bias)
    stats_ref[...] = jnp.zeros_like(stats_ref)
    for h in range(GROUP_HEADS):
        kh = joined(slots, 0, head(h))
        vh = joined(slots, 1, head(h))
        scores = mm(kh, q_ref[:, head(h)], NT) * SCALE + bias[...]
        top = jnp.floor(jnp.max(scores, axis=0, keepdims=True) * 0.125) * 8.0
        expo = jnp.exp(scores - top)
        att[head(h), :] = mm(vh, expo.astype(BF16), TN)
        dots = jnp.sum(expo * mm(vh, d_ref[head(h), :], NN), axis=0, keepdims=True)
        stats_ref[0, h : h + 1, :] = top
        stats_ref[1, h : h + 1, :] = jnp.sum(expo, axis=0, keepdims=True)
        stats_ref[2, h : h + 1, :] = dots
    halve(place, att, pieces, keep_ref, send_ref)


def row_weights(spread, piece, rows_each):
    q_len = spread.shape[1]
    row = lax.broadcasted_iota(jnp.int32, (rows_each, q_len), 0)
    before = spread[pl.ds(piece + 7, 1), :]
    after = spread[pl.ds(piece + 8, 1), :]
    return jnp.where(row < (HEAD_DIM - rows_each) * piece, before, after)


def core_kernel(place, keep_ref, stats_ref, got_ref, got_stats_ref, o0, o1, o2, o3, spread, payload):
    pair, core = place[1], place[2]
    rows_each = keep_ref.shape[1]
    top = jnp.maximum(stats_ref[0], got_stats_ref[0])
    mine, other = jnp.exp(stats_ref[0] - top), jnp.exp(got_stats_ref[0] - top)
    total = mine * stats_ref[1] + other * got_stats_ref[1]
    dots = mine * stats_ref[2] + other * got_stats_ref[2]
    total_hi, dots_hi = total.astype(BF16).astype(F32), dots.astype(BF16).astype(F32)
    tail = jnp.concatenate([top, total_hi, total - total_hi, dots_hi, dots - dots_hi], axis=0)
    spread[...] = jnp.zeros_like(spread)
    spread[0, 8:16, :] = mine
    spread[1, 8:16, :] = other
    for b in range(GROUPS):
        piece = 2 * b + core
        payload[b, 80:88, :] = jnp.zeros_like(top)
        payload[b, :rows_each, :] = row_weights(spread.at[0], piece, rows_each) * keep_ref[b] + row_weights(
            spread.at[1], piece, rows_each
        ) * got_ref[b].astype(F32)
        payload[b, 88:, :] = tail
    for j, out in enumerate((o0, o1, o2, o3)):
        out[...] = payload[lax.bitwise_xor(pair, j)].astype(BF16)


def read_stats(parts):
    tops = [p[88:96, :].astype(F32) for p in parts]
    top = functools.reduce(jnp.maximum, tops)
    scaled = [jnp.exp(t - top) for t in tops]
    total = sum(w * (p[96:104].astype(F32) + p[104:112].astype(F32)) for w, p in zip(scaled, parts))
    inverse = 1.0 / jnp.where(total > 0.0, total, 1.0)
    dots = sum(w * (p[112:120].astype(F32) + p[120:128].astype(F32)) for w, p in zip(scaled, parts)) * inverse
    return top, inverse, dots, scaled


def attended_kernel(place, p0, p1, p2, p3, out_ref, spread):
    rows_each = out_ref.shape[0]
    parts = [p[...].astype(F32) for p in (p0, p1, p2, p3)]
    _, inverse, _, scaled = read_stats(parts)
    spread[...] = jnp.zeros_like(spread)
    total = jnp.zeros(out_ref.shape, F32)
    for j, part in enumerate(parts):
        spread[j, 8:16, :] = scaled[j] * inverse
        total += row_weights(spread.at[j], 2 * place[1] + place[2], rows_each) * part[:rows_each]
    out_ref[...] = total.astype(BF16)


def backward_kernel(
    place, ws_ref, q_ref, s0, s1, s2, s3, d_ref, p0, p1, p2, p3, o0, o1, o2, o3, keep_ref, send_ref, bias, gq, pieces, stats
):
    kv_len = s0.shape[1]
    slots = (s0, s1, s2, s3)
    set_mask(place, ws_ref, bias)
    stats[0], stats[1], stats[2], _ = read_stats([p[...].astype(F32) for p in (p0, p1, p2, p3)])
    for h in range(GROUP_HEADS):
        kh = joined(slots, 0, head(h))
        vh = joined(slots, 1, head(h))
        qh = q_ref[:, head(h)]
        dh = d_ref[head(h), :]
        scores = mm(kh, qh, NT) * SCALE + bias[...]
        probs = jnp.exp(scores - stats[0, h : h + 1, :]) * stats[1, h : h + 1, :]
        dscores = probs * (mm(vh, dh, NN) - stats[2, h : h + 1, :])
        probs = probs.astype(BF16)
        dscores = dscores.astype(BF16)
        gk = (mm(dscores, qh, NN) * SCALE).astype(BF16)
        gv = mm(probs, dh, NT).astype(BF16)
        for s, out in enumerate((o0, o1, o2, o3)):
            part = slice(s * kv_len, (s + 1) * kv_len)
            out[0, :, head(h)] = gk[part]
            out[1, :, head(h)] = gv[part]
        gq[head(h), :] = mm(kh, dscores, TN) * SCALE
    halve(place, gq, pieces, keep_ref, send_ref)


def add_kernel(place, keep_ref, got_ref, o0, o1, o2, o3, pieces):
    for b in range(GROUPS):
        pieces[b] = keep_ref[b] + got_ref[b].astype(F32)
    for j, out in enumerate((o0, o1, o2, o3)):
        out[...] = pieces[lax.bitwise_xor(place[1], j)].astype(BF16)


def weight_kernel(att_ref, cot_ref, out_ref, full):
    pieces, _, width = out_ref.shape
    full[...] = mm(att_ref[...], cot_ref[...], NT)
    for s in range(pieces):
        out_ref[s] = full[:, s * width : (s + 1) * width].astype(BF16)


def sum_kernel(x_ref, out_ref):
    out_ref[...] = sum(x_ref[j].astype(F32) for j in range(x_ref.shape[0])).astype(BF16)


def add4_kernel(x0, x1, x2, x3, out_ref):
    out_ref[...] = sum(x[...].astype(F32) for x in (x0, x1, x2, x3)).astype(BF16)


SMEM = pl.BlockSpec(memory_space=pltpu.SMEM)
WHOLE = pl.BlockSpec(memory_space=pltpu.VMEM)


def call(name, kernel, n_in, out_shapes, scratch=(), scalars=1, grid=(), in_blocks=None, out_blocks=None):
    return pl.pallas_call(
        kernel,
        out_shape=out_shapes,
        grid=grid,
        in_specs=[SMEM] * scalars + (in_blocks or [WHOLE] * n_in),
        out_specs=out_blocks or jax.tree.map(lambda _: WHOLE, out_shapes),
        scratch_shapes=list(scratch),
        compiler_params=pltpu.CompilerParams(vmem_limit_bytes=VMEM_LIMIT),
        cost_estimate=pl.CostEstimate(flops=int(COST[name] * 1e9), bytes_accessed=0, transcendentals=0),
        name=name,
    )


def rows_block(shape, dim):
    block = tuple(n // 4 if d == dim else n for d, n in enumerate(shape))
    return pl.BlockSpec(block, lambda i: tuple(i if d == dim else 0 for d in range(len(shape))))


ALL = [(a, b) for a in range(GROUPS) for b in range(GROUPS)]


def swap_chip(x, s):
    return lax.ppermute(x, ("zl", "x_lo"), [(i, i ^ s) for i in range(GROUPS)])


def swap_pair(x, j):
    return lax.ppermute(x, "zp", [(i, i ^ j) for i in range(GROUPS)])


def swap_core(x):
    return lax.ppermute(x, "core", [(0, 1), (1, 0)])


def to_holder(x, j):
    return lax.ppermute(x, ("zp", "zl", "x_lo"), [(a * GROUPS + b, (b ^ j) * GROUPS + a) for a, b in ALL])


def to_owner(x, j):
    return lax.ppermute(x, ("zp", "zl", "x_lo"), [((b ^ j) * GROUPS + a, a * GROUPS + b) for a, b in ALL])


def local(queries, keys, values, out_grad, w_out, window_start):
    query, key_rows, value_rows, cotangent = queries[0], keys[0], values[0], out_grad[0].T
    q_len = query.shape[0]
    kv_len, width = key_rows.shape
    rows_each, model = w_out.shape
    sections = lax.axis_size("section")
    place = jnp.stack([lax.axis_index(("zl", "x_lo")), lax.axis_index("zp"), lax.axis_index("core")]).astype(jnp.int32)
    starts = window_start.reshape(1, q_len)
    sds = jax.ShapeDtypeStruct
    four = range(GROUPS)
    slots4 = [sds((2, kv_len, GROUP_WIDTH), BF16)] * GROUPS
    halves = [sds((GROUPS, rows_each, q_len), F32), sds((GROUPS, rows_each, q_len), BF16)]
    bias = pltpu.VMEM((GROUPS * kv_len, q_len), F32)
    features = pltpu.VMEM((GROUP_WIDTH, q_len), F32)
    pieces = pltpu.VMEM((PIECES, rows_each, q_len), F32)

    cut = [rows_block((2, kv_len, GROUP_WIDTH), 1)] * GROUPS
    *send, q_own = call(
        "pack",
        pack_kernel,
        3,
        slots4 + [sds((q_len, GROUP_WIDTH), BF16)],
        grid=(4,),
        in_blocks=[rows_block(x.shape, 0) for x in (key_rows, value_rows, query)],
        out_blocks=cut + [rows_block((q_len, GROUP_WIDTH), 0)],
    )(place, key_rows, value_rows, query)
    w_out, send = lax.optimization_barrier((w_out, send))
    slots = [send[0]] + [swap_chip(send[s], s) for s in range(1, GROUPS)]
    d_own = lax.dot_general(w_out, cotangent, NN, preferred_element_type=F32).astype(BF16)
    mine = [to_holder(d_own, j) for j in four]
    theirs = swap_core(jnp.stack(mine))
    d_group = call("join", join_kernel, 5, sds((GROUP_WIDTH, q_len), BF16), [pieces, features])(place, *mine, theirs)

    keep, half, stats = call(
        "forward", forward_kernel, 7, halves + [sds((3, 8, q_len), F32)], [bias, features, pieces]
    )(place, starts, q_own, *slots, d_group)
    parts = call(
        "core",
        core_kernel,
        4,
        [sds((128, q_len), BF16)] * GROUPS,
        [pltpu.VMEM((2, 24, q_len), F32), pltpu.VMEM((GROUPS, 128, q_len), F32)],
    )(place, keep, stats, swap_core(half), swap_core(stats))
    parts = [parts[0]] + [swap_pair(parts[j], j) for j in range(1, GROUPS)]
    attended = call(
        "attended", attended_kernel, 4, sds((rows_each, q_len), BF16), [pltpu.VMEM((GROUPS, 24, q_len), F32)]
    )(place, *parts)
    attended, parts = lax.optimization_barrier((attended, parts))
    attended = to_owner(attended, 0)

    *back, keep, half = call(
        "backward", backward_kernel, 11, slots4 + halves, [bias, features, pieces, pltpu.VMEM((3, 8, q_len), F32)]
    )(place, starts, q_own, *slots, d_group, *parts)
    attended, keep = lax.optimization_barrier((attended, keep))
    back = [back[0]] + [swap_chip(back[s], s) for s in range(1, GROUPS)]

    part = model // sections
    gw = call(
        "weight", weight_kernel, 2, sds((sections, rows_each, part), BF16), [pltpu.VMEM((rows_each, model), F32)], scalars=0
    )(attended, cotangent)
    gw = lax.all_to_all(gw, "section", 0, 0)

    gq = call("add", add_kernel, 2, [sds((rows_each, q_len), BF16)] * GROUPS, [pltpu.VMEM((GROUPS, rows_each, q_len), F32)])(
        place, keep, swap_core(half)
    )
    gq = [to_owner(gq[j], j) for j in four]

    grad_weight = call("sum", sum_kernel, 1, sds((rows_each, part), BF16), scalars=0)(gw)
    grad_weight, back = lax.optimization_barrier((grad_weight, back))
    grad_k, grad_v = call(
        "unpack",
        unpack_kernel,
        4,
        [sds((kv_len, width), BF16)] * 2,
        grid=(4,),
        in_blocks=cut,
        out_blocks=[rows_block((kv_len, width), 0)] * 2,
    )(place, *back)
    grad_q = call("add4", add4_kernel, 4, sds((rows_each, q_len), BF16), scalars=0)(*gq)
    return grad_q[None], grad_k[None], grad_v[None], grad_weight


def solution(mesh):
    sections = mesh.shape["section"]
    fine = Mesh(mesh.devices.reshape(sections, GROUPS, 2, 2, 2), ("section",) + SEQ_AXES)
    return jax.shard_map(
        local,
        mesh=fine,
        in_specs=(
            P("section", None, None),
            P("section", SEQ_AXES, None),
            P("section", SEQ_AXES, None),
            P("section", None, None),
            P(SEQ_AXES, None),
            P(),
        ),
        out_specs=(
            P("section", SEQ_AXES, None),
            P("section", SEQ_AXES, None),
            P("section", SEQ_AXES, None),
            P(SEQ_AXES, "section"),
        ),
        check_vma=False,
    )
```

```python
import functools

import jax
import jax.numpy as jnp
from jax import lax
from jax.experimental import pallas as pl
from jax.experimental.pallas import tpu as pltpu
from jax.sharding import Mesh, PartitionSpec as P

HEADS = 28
HEAD_DIM = 96
GROUPS = 4
GROUP_HEADS = HEADS // GROUPS
GROUP_WIDTH = GROUP_HEADS * HEAD_DIM
PIECES = 8
NEG = -(2.0**99)
ATT, CENTRED, PLAIN, STATS = 0, 88, 176, 264
SCALE = HEAD_DIM ** (-0.5)
SECTION_AXES = ("x_hi", "y")
SEQ_AXES = ("zp", "zl", "x_lo", "core")
F32 = jnp.float32
BF16 = jnp.bfloat16
VMEM_LIMIT = 48 * 1024 * 1024
SMALL_LIMIT = 16 * 1024 * 1024
COST = dict(
    pack=1, join=1, forward=2, core=1, finish=1, backward=3, weight=2, unpack=10, sum_y=0, sum=0
)
NT = (((1,), (1,)), ((), ()))
NN = (((1,), (0,)), ((), ()))
TN = (((0,), (0,)), ((), ()))


def mm(a, b, dims):
    return lax.dot_general(a, b, dims, preferred_element_type=F32)


def pack_kernel(place, k_hbm, v_hbm, q_hbm, o0, o1, o2, o3, q_ref, k_all, v_all, q_all, sems):
    chip = place[0]
    copies = [
        pltpu.make_async_copy(src, dst, sems.at[n]) for n, (src, dst) in enumerate(((k_hbm, k_all), (v_hbm, v_all), (q_hbm, q_all)))
    ]
    for copy in copies:
        copy.start()
    for n, copy in enumerate(copies):
        copy.wait()
        for g in range(GROUPS):
            cols = slice(g * GROUP_WIDTH, (g + 1) * GROUP_WIDTH)
            for s, out in enumerate((o0, o1, o2, o3)):
                if n < 2:

                    @pl.when(lax.bitwise_xor(chip, s) == g)
                    def _():
                        out[n] = (k_all, v_all)[n][:, cols]

            if n == 2:

                @pl.when(chip == g)
                def _():
                    q_ref[...] = q_all[:, cols]


def unpack_kernel(place, s0, s1, s2, s3, gk_ref, gv_ref, all_k, all_v, sems):
    chip = place[0]
    slots = (s0, s1, s2, s3)
    copies = []
    for n, (rows, out) in enumerate(((all_k, gk_ref), (all_v, gv_ref))):
        for g in range(GROUPS):
            cols = slice(g * GROUP_WIDTH, (g + 1) * GROUP_WIDTH)
            for s in range(GROUPS):

                @pl.when(lax.bitwise_xor(chip, s) == g)
                def _():
                    rows[:, cols] = slots[s][n]

        copies.append(pltpu.make_async_copy(rows, out, sems.at[n]))
        copies[-1].start()
    for copy in copies:
        copy.wait()


def set_mask(place, ws_ref, bias):
    chip, pair, half = place[0], place[1], place[2]
    q_len = ws_ref.shape[1]
    kv_len = bias.shape[0] // GROUPS
    context = kv_len * GROUPS * PIECES
    rows = lax.broadcasted_iota(jnp.int32, (kv_len, q_len), 0)
    query_pos = context - q_len + lax.broadcasted_iota(jnp.int32, (kv_len, q_len), 1)
    for s in range(GROUPS):
        owner = pair * PIECES + 2 * lax.bitwise_xor(chip, s) + half
        key_pos = owner * kv_len + rows
        visible = (key_pos >= ws_ref[...]) & (key_pos <= query_pos)
        bias[s * kv_len : (s + 1) * kv_len, :] = jnp.where(visible, 0.0, NEG)


def join_kernel(place, m0, m1, m2, m3, theirs_ref, out_ref, pieces, rows):
    pair, half = place[1], place[2]
    rows_each = m0.shape[0]
    for j, mine in enumerate((m0, m1, m2, m3)):
        at = lax.bitwise_xor(pair, j)
        pieces[2 * at + half] = mine[...].astype(F32)
        pieces[2 * at + 1 - half] = theirs_ref[j].astype(F32)
    for k in range(PIECES):
        rows[k * rows_each : (k + 1) * rows_each, :] = pieces[k]
    out_ref[...] = rows[...].astype(BF16)


def head(h):
    return slice(h * HEAD_DIM, (h + 1) * HEAD_DIM)


def joined(slots, which, cols):
    return jnp.concatenate([s[which, :, cols] for s in slots], axis=0)


def halve(place, full, pieces, at, keep_ref, send_ref):
    half = place[2]
    rows_each = pieces.shape[1]
    for k in range(PIECES):
        pieces[k] = full[k * rows_each : (k + 1) * rows_each, :]
    for b in range(GROUPS):
        keep_ref[at * GROUPS + b] = pieces[2 * b + half]
        send_ref[at * GROUPS + b] = pieces[2 * b + 1 - half].astype(BF16)


def forward_kernel(
    place, ws_ref, q_ref, s0, s1, s2, s3, d_ref, keep_ref, send_ref, stats_ref, bias, att, centred, plain, pieces
):
    slots = (s0, s1, s2, s3)
    set_mask(place, ws_ref, bias)
    stats_ref[...] = jnp.zeros_like(stats_ref)
    for h in range(GROUP_HEADS):
        kh = joined(slots, 0, head(h))
        vh = joined(slots, 1, head(h))
        scores = mm(kh, q_ref[:, head(h)], NT) * SCALE + bias[...]
        top = jnp.floor(jnp.max(scores, axis=0, keepdims=True) * 0.125) * 8.0
        expo = jnp.exp(scores - top)
        total = jnp.sum(expo, axis=0, keepdims=True)
        dprobs = mm(vh, d_ref[head(h), :], NN)
        dots = jnp.sum(expo * dprobs, axis=0, keepdims=True) / total
        expo_b = expo.astype(BF16)
        att[head(h), :] = mm(vh, expo_b, TN)
        plain[head(h), :] = mm(kh, expo_b, TN)
        centred[head(h), :] = mm(kh, (expo * (dprobs - dots)).astype(BF16), TN)
        stats_ref[0, h : h + 1, :] = top
        stats_ref[1, h : h + 1, :] = total
        stats_ref[2, h : h + 1, :] = dots
    for at, full in enumerate((att, centred, plain)):
        halve(place, full, pieces, at, keep_ref, send_ref)


def row_weights(spread, piece, rows_each):
    q_len = spread.shape[1]
    row = lax.broadcasted_iota(jnp.int32, (rows_each, q_len), 0)
    before = spread[pl.ds(piece + 7, 1), :]
    after = spread[pl.ds(piece + 8, 1), :]
    return jnp.where(row < (HEAD_DIM - rows_each) * piece, before, after)


def merged(stats):
    top = functools.reduce(jnp.maximum, [s[0] for s in stats])
    weights = [jnp.exp(s[0] - top) for s in stats]
    total = sum(w * s[1] for w, s in zip(weights, stats))
    total = jnp.where(total > 0.0, total, 1.0)
    dots = sum(w * s[1] * s[2] for w, s in zip(weights, stats)) / total
    return top, total, dots, weights, [dots - s[2] for s in stats]


def core_kernel(place, keep_ref, stats_ref, got_ref, got_stats_ref, o0, o1, o2, o3, spread, payload):
    pair, half = place[1], place[2]
    rows_each = keep_ref.shape[1]
    top, total, dots, weights, shifts = merged([[r[n] for n in range(3)] for r in (stats_ref, got_stats_ref)])
    total_hi, dots_hi = total.astype(BF16).astype(F32), dots.astype(BF16).astype(F32)
    tail = jnp.concatenate([top, total_hi, total - total_hi, dots_hi, dots - dots_hi], axis=0)
    spread[...] = jnp.zeros_like(spread)
    for n in range(2):
        spread[n, 8:16, :] = weights[n]
        spread[2 + n, 8:16, :] = weights[n] * shifts[n]
    payload[...] = jnp.zeros_like(payload)
    for b in range(GROUPS):
        w0, w1, c0, c1 = [row_weights(spread.at[n], 2 * b + half, rows_each) for n in range(4)]
        plain0, plain1 = keep_ref[2 * GROUPS + b], got_ref[2 * GROUPS + b].astype(F32)
        payload[b, ATT : ATT + rows_each, :] = w0 * keep_ref[b] + w1 * got_ref[b].astype(F32)
        payload[b, CENTRED : CENTRED + rows_each, :] = (
            w0 * keep_ref[GROUPS + b] + w1 * got_ref[GROUPS + b].astype(F32) - c0 * plain0 - c1 * plain1
        )
        payload[b, PLAIN : PLAIN + rows_each, :] = w0 * plain0 + w1 * plain1
        payload[b, STATS:, :] = tail
    for j, out in enumerate((o0, o1, o2, o3)):
        out[...] = payload[lax.bitwise_xor(pair, j)].astype(BF16)


def read_stats(parts):
    tails = [p[STATS:, :].astype(F32) for p in parts]
    return merged([[t[0:8], t[8:16] + t[16:24], t[24:32] + t[32:40]] for t in tails])


def finish_kernel(place, p0, p1, p2, p3, out_ref, spread):
    rows_each = out_ref.shape[1]
    parts = (p0, p1, p2, p3)
    _, total, _, weights, shifts = read_stats(parts)
    spread[...] = jnp.zeros_like(spread)
    att = jnp.zeros(out_ref.shape[1:], F32)
    grad = jnp.zeros(out_ref.shape[1:], F32)
    for n, part in enumerate(parts):
        spread[0, 8:16, :] = weights[n] / total
        spread[1, 8:16, :] = weights[n] / total * shifts[n]
        w, c = [row_weights(spread.at[m], 2 * place[1] + place[2], rows_each) for m in range(2)]
        rows = part[...].astype(F32)
        att += w * rows[ATT : ATT + rows_each]
        grad += w * rows[CENTRED : CENTRED + rows_each] - c * rows[PLAIN : PLAIN + rows_each]
    out_ref[0] = att.astype(BF16)
    out_ref[1] = (grad * SCALE).astype(BF16)


def backward_kernel(place, ws_ref, q_ref, s0, s1, s2, s3, d_ref, p0, p1, p2, p3, o0, o1, o2, o3, bias, stats):
    kv_len = s0.shape[1]
    slots = (s0, s1, s2, s3)
    set_mask(place, ws_ref, bias)
    top, total, dots, _, _ = read_stats((p0, p1, p2, p3))
    stats[0], stats[1], stats[2] = top, 1.0 / total, dots
    for h in range(GROUP_HEADS):
        kh = joined(slots, 0, head(h))
        vh = joined(slots, 1, head(h))
        qh = q_ref[:, head(h)]
        dh = d_ref[head(h), :]
        scores = mm(kh, qh, NT) * SCALE + bias[...]
        probs = jnp.exp(scores - stats[0, h : h + 1, :]) * stats[1, h : h + 1, :]
        dscores = (probs * (mm(vh, dh, NN) - stats[2, h : h + 1, :])).astype(BF16)
        gk = (mm(dscores, qh, NN) * SCALE).astype(BF16)
        gv = mm(probs.astype(BF16), dh, NT).astype(BF16)
        for s, out in enumerate((o0, o1, o2, o3)):
            part = slice(s * kv_len, (s + 1) * kv_len)
            out[0, :, head(h)] = gk[part]
            out[1, :, head(h)] = gv[part]


def weight_kernel(rows_ref, cot_ref, out_ref, gq_ref, full):
    pieces, _, width = out_ref.shape
    full[...] = mm(rows_ref[0], cot_ref[...], NT)
    gq_ref[...] = rows_ref[1]
    for s in range(pieces):
        x_hi, y = divmod(s, pieces // 2)
        out_ref[2 * y + x_hi] = full[:, s * width : (s + 1) * width].astype(BF16)


def sum_y_kernel(place, x_ref, keep_ref, send_ref):
    x_hi = place[3]
    half = x_ref.shape[0] // 2
    keep_ref[...] = sum(x_ref[2 * y + x_hi].astype(F32) for y in range(half))
    send_ref[...] = sum(x_ref[2 * y + 1 - x_hi].astype(F32) for y in range(half)).astype(BF16)


def sum_kernel(keep_ref, got_ref, out_ref):
    out_ref[...] = (keep_ref[...] + got_ref[...].astype(F32)).astype(BF16)


SMEM = pl.BlockSpec(memory_space=pltpu.SMEM)
ANY = pl.BlockSpec(memory_space=pl.ANY)
WHOLE = pl.BlockSpec(memory_space=pltpu.VMEM)


def call(name, kernel, n_in, out_shapes, scratch=(), scalars=1, in_blocks=None, out_blocks=None, limit=VMEM_LIMIT):
    return pl.pallas_call(
        kernel,
        out_shape=out_shapes,
        in_specs=[SMEM] * scalars + (in_blocks or [WHOLE] * n_in),
        out_specs=out_blocks or jax.tree.map(lambda _: WHOLE, out_shapes),
        scratch_shapes=list(scratch),
        compiler_params=pltpu.CompilerParams(vmem_limit_bytes=limit),
        cost_estimate=pl.CostEstimate(flops=int(COST[name] * 1e9), bytes_accessed=0, transcendentals=0),
        name=name,
    )


def swap_chip(x, s):
    return lax.ppermute(x, ("zl", "x_lo"), [(i, i ^ s) for i in range(GROUPS)])


def swap_pair(x, j):
    return lax.ppermute(x, "zp", [(i, i ^ j) for i in range(GROUPS)])


def swap_half(x):
    return lax.ppermute(x, "core", [(0, 1), (1, 0)])


def trade(x, j=0):
    return lax.ppermute(x, ("zp", "zl", "x_lo"), [(a * GROUPS + b, (b ^ j) * GROUPS + a) for a in range(GROUPS) for b in range(GROUPS)])


def local(queries, keys, values, out_grad, w_out, window_start):
    query, key_rows, value_rows, cotangent = queries[0], keys[0], values[0], out_grad[0].T
    q_len = query.shape[0]
    kv_len, width = key_rows.shape
    rows_each, model = w_out.shape
    sections = lax.axis_size(SECTION_AXES)
    place = jnp.stack([lax.axis_index(("zl", "x_lo")), lax.axis_index("zp"), lax.axis_index("core"), lax.axis_index("x_hi")]).astype(jnp.int32)
    starts = window_start.reshape(1, q_len)
    sds = jax.ShapeDtypeStruct
    slots4 = [sds((2, kv_len, GROUP_WIDTH), BF16)] * GROUPS
    bias = pltpu.VMEM((GROUPS * kv_len, q_len), F32)
    features = pltpu.VMEM((GROUP_WIDTH, q_len), F32)
    pieces = pltpu.VMEM((PIECES, rows_each, q_len), F32)

    whole = pltpu.VMEM((kv_len, width), BF16)
    *send, q_own = call(
        "pack",
        pack_kernel,
        3,
        slots4 + [sds((q_len, GROUP_WIDTH), BF16)],
        [whole, whole, pltpu.VMEM((q_len, width), BF16), pltpu.SemaphoreType.DMA((3,))],
        in_blocks=[ANY] * 3,
        limit=60 * 1024 * 1024,
    )(place, key_rows, value_rows, query)
    w_out, send = lax.optimization_barrier((w_out, send))
    slots = [send[0]] + [swap_chip(send[s], s) for s in range(1, GROUPS)]
    d_own = lax.dot_general(w_out, cotangent, NN, preferred_element_type=F32).astype(BF16)
    mine = [trade(d_own, j) for j in range(GROUPS)]
    theirs = swap_half(jnp.stack(mine))
    d_group = call("join", join_kernel, 5, sds((GROUP_WIDTH, q_len), BF16), [pieces, features])(place, *mine, theirs)

    keep, half, stats = call(
        "forward",
        forward_kernel,
        7,
        [sds((3 * GROUPS, rows_each, q_len), F32), sds((3 * GROUPS, rows_each, q_len), BF16), sds((3, 8, q_len), F32)],
        [bias, features, features, features, pieces],
    )(place, starts, q_own, *slots, d_group)
    parts = call(
        "core",
        core_kernel,
        4,
        [sds((STATS + 40, q_len), BF16)] * GROUPS,
        [pltpu.VMEM((4, 24, q_len), F32), pltpu.VMEM((GROUPS, STATS + 40, q_len), F32)],
    )(place, keep, stats, swap_half(half), swap_half(stats))
    parts = [parts[0]] + [swap_pair(parts[j], j) for j in range(1, GROUPS)]
    rows = call("finish", finish_kernel, 4, sds((2, rows_each, q_len), BF16), [pltpu.VMEM((2, 24, q_len), F32)])(place, *parts)
    rows, parts = lax.optimization_barrier((rows, parts))
    rows = trade(rows)

    back = call("backward", backward_kernel, 11, slots4, [bias, pltpu.VMEM((3, 8, q_len), F32)])(
        place, starts, q_own, *slots, d_group, *parts
    )
    rows, back = lax.optimization_barrier((rows, back))
    back = [back[0]] + [swap_chip(back[s], s) for s in range(1, GROUPS)]

    part = model // sections
    gw, grad_q = call(
        "weight",
        weight_kernel,
        2,
        [sds((sections, rows_each, part), BF16), sds((rows_each, q_len), BF16)],
        [pltpu.VMEM((rows_each, model), F32)],
        scalars=0,
        limit=SMALL_LIMIT,
    )(rows, cotangent)
    gw = lax.all_to_all(gw, "y", 0, 0, tiled=True)
    grad_k, grad_v = call(
        "unpack",
        unpack_kernel,
        4,
        [sds((kv_len, width), BF16)] * 2,
        [whole, whole, pltpu.SemaphoreType.DMA((2,))],
        out_blocks=[ANY] * 2,
    )(place, *back)
    gw, grad_k = lax.optimization_barrier((gw, grad_k))
    keep, half = call("sum_y", sum_y_kernel, 1, [sds((rows_each, part), F32), sds((rows_each, part), BF16)], limit=SMALL_LIMIT)(place, gw)
    half = lax.ppermute(half, "x_hi", [(0, 1), (1, 0)])
    grad_weight = call("sum", sum_kernel, 2, sds((rows_each, part), BF16), scalars=0, limit=SMALL_LIMIT)(keep, half)
    return grad_q[None], grad_k[None], grad_v[None], grad_weight


def solution(mesh):
    fine = Mesh(mesh.devices.reshape(2, mesh.shape["section"] // 2, GROUPS, 2, 2, 2), SECTION_AXES + SEQ_AXES)
    return jax.shard_map(
        local,
        mesh=fine,
        in_specs=(
            P(SECTION_AXES, None, None),
            P(SECTION_AXES, SEQ_AXES, None),
            P(SECTION_AXES, SEQ_AXES, None),
            P(SECTION_AXES, None, None),
            P(SEQ_AXES, None),
            P(),
        ),
        out_specs=(
            P(SECTION_AXES, SEQ_AXES, None),
            P(SECTION_AXES, SEQ_AXES, None),
            P(SECTION_AXES, SEQ_AXES, None),
            P(SEQ_AXES, SECTION_AXES),
        ),
        check_vma=False,
    )
```

```python
import functools

import jax
import jax.numpy as jnp
from jax import lax
from jax.experimental import pallas as pl
from jax.experimental.pallas import tpu as pltpu
from jax.sharding import Mesh, PartitionSpec as P

HEADS = 28
HEAD_DIM = 96
GROUPS = 4
GROUP_HEADS = HEADS // GROUPS
GROUP_WIDTH = GROUP_HEADS * HEAD_DIM
PIECES = 8
NEG = -(2.0**99)
ATT, CENTRED, PLAIN, STATS = 0, 88, 176, 264
SCALE = HEAD_DIM ** (-0.5)
SECTION_AXES = ("x_hi", "y")
SEQ_AXES = ("zp", "zl", "x_lo", "core")
F32 = jnp.float32
BF16 = jnp.bfloat16
VMEM_LIMIT = 32 * 1024 * 1024
SMALL_LIMIT = 16 * 1024 * 1024
COST = dict(
    pack=1, join=1, forward=2, core=1, finish=1, backward=3, weight=2, unpack_k=10, unpack_v=3, sum_y=0, sum=0
)
NT = (((1,), (1,)), ((), ()))
NN = (((1,), (0,)), ((), ()))
TN = (((0,), (0,)), ((), ()))


def mm(a, b, dims):
    return lax.dot_general(a, b, dims, preferred_element_type=F32)


def pack_kernel(place, k_hbm, v_hbm, q_hbm, o0, o1, o2, o3, q_ref, k_all, v_all, q_all, sems):
    chip = place[0]
    copies = [
        pltpu.make_async_copy(src, dst, sems.at[n]) for n, (src, dst) in enumerate(((k_hbm, k_all), (v_hbm, v_all), (q_hbm, q_all)))
    ]
    for copy in copies:
        copy.start()
    for n, copy in enumerate(copies):
        copy.wait()
        for g in range(GROUPS):
            cols = slice(g * GROUP_WIDTH, (g + 1) * GROUP_WIDTH)
            for s, out in enumerate((o0, o1, o2, o3)):
                if n < 2:

                    @pl.when(lax.bitwise_xor(chip, s) == g)
                    def _():
                        out[n] = (k_all, v_all)[n][:, cols]

            if n == 2:

                @pl.when(chip == g)
                def _():
                    q_ref[...] = q_all[:, cols]


def unpack_kernel(which, place, s0, s1, s2, s3, out_ref, rows, sem):
    chip = place[0]
    for g in range(GROUPS):
        cols = slice(g * GROUP_WIDTH, (g + 1) * GROUP_WIDTH)
        for s, slot in enumerate((s0, s1, s2, s3)):

            @pl.when(lax.bitwise_xor(chip, s) == g)
            def _():
                rows[:, cols] = slot[which]

    copy = pltpu.make_async_copy(rows, out_ref, sem)
    copy.start()
    copy.wait()


def set_mask(place, ws_ref, bias):
    chip, pair, half = place[0], place[1], place[2]
    q_len = ws_ref.shape[1]
    kv_len = bias.shape[0] // GROUPS
    context = kv_len * GROUPS * PIECES
    rows = lax.broadcasted_iota(jnp.int32, (kv_len, q_len), 0)
    query_pos = context - q_len + lax.broadcasted_iota(jnp.int32, (kv_len, q_len), 1)
    for s in range(GROUPS):
        owner = pair * PIECES + 2 * lax.bitwise_xor(chip, s) + half
        key_pos = owner * kv_len + rows
        visible = (key_pos >= ws_ref[...]) & (key_pos <= query_pos)
        bias[s * kv_len : (s + 1) * kv_len, :] = jnp.where(visible, 0.0, NEG)


def join_kernel(place, m0, m1, t0, t1, out_ref, pieces, rows):
    pair, half = place[1], place[2]
    rows_each = m0.shape[1]
    for j, (mine, theirs) in enumerate(((m0, t0), (m1, t1))):
        at = 2 * lax.bitwise_xor(pair, 2 * half + j)
        pieces[at + half] = mine[0].astype(F32)
        pieces[at + 1 - half] = mine[1].astype(F32)
        at = 2 * lax.bitwise_xor(pair, 2 * (1 - half) + j)
        pieces[at + 1 - half] = theirs[0].astype(F32)
        pieces[at + half] = theirs[1].astype(F32)
    for k in range(PIECES):
        rows[k * rows_each : (k + 1) * rows_each, :] = pieces[k]
    out_ref[...] = rows[...].astype(BF16)


def head(h):
    return slice(h * HEAD_DIM, (h + 1) * HEAD_DIM)


def joined(slots, which, cols):
    return jnp.concatenate([s[which, :, cols] for s in slots], axis=0)


def halve(place, full, pieces, at, keep_ref, send_ref):
    half = place[2]
    rows_each = pieces.shape[1]
    for k in range(PIECES):
        pieces[k] = full[k * rows_each : (k + 1) * rows_each, :]
    for b in range(GROUPS):
        keep_ref[at * GROUPS + b] = pieces[2 * b + half]
        send_ref[at * GROUPS + b] = pieces[2 * b + 1 - half].astype(BF16)


def forward_kernel(
    place, ws_ref, q_ref, s0, s1, s2, s3, d_ref, keep_ref, send_ref, stats_ref, bias, att, centred, plain, pieces
):
    slots = (s0, s1, s2, s3)
    set_mask(place, ws_ref, bias)
    stats_ref[...] = jnp.zeros_like(stats_ref)
    for h in range(GROUP_HEADS):
        kh = joined(slots, 0, head(h))
        vh = joined(slots, 1, head(h))
        scores = mm(kh, q_ref[:, head(h)], NT) * SCALE + bias[...]
        top = jnp.floor(jnp.max(scores, axis=0, keepdims=True) * 0.125) * 8.0
        expo = jnp.exp(scores - top)
        total = jnp.sum(expo, axis=0, keepdims=True)
        dprobs = mm(vh, d_ref[head(h), :], NN)
        dots = jnp.sum(expo * dprobs, axis=0, keepdims=True) / total
        expo_b = expo.astype(BF16)
        att[head(h), :] = mm(vh, expo_b, TN)
        plain[head(h), :] = mm(kh, expo_b, TN)
        centred[head(h), :] = mm(kh, (expo * (dprobs - dots)).astype(BF16), TN)
        stats_ref[0, h : h + 1, :] = top
        stats_ref[1, h : h + 1, :] = total
        stats_ref[2, h : h + 1, :] = dots
    for at, full in enumerate((att, centred, plain)):
        halve(place, full, pieces, at, keep_ref, send_ref)


def row_weights(spread, piece, rows_each):
    q_len = spread.shape[1]
    row = lax.broadcasted_iota(jnp.int32, (rows_each, q_len), 0)
    before = spread[pl.ds(piece + 7, 1), :]
    after = spread[pl.ds(piece + 8, 1), :]
    return jnp.where(row < (HEAD_DIM - rows_each) * piece, before, after)


def merged(stats):
    top = functools.reduce(jnp.maximum, [s[0] for s in stats])
    weights = [jnp.exp(s[0] - top) for s in stats]
    total = sum(w * s[1] for w, s in zip(weights, stats))
    total = jnp.where(total > 0.0, total, 1.0)
    dots = sum(w * s[1] * s[2] for w, s in zip(weights, stats)) / total
    return top, total, dots, weights, [dots - s[2] for s in stats]


def core_kernel(place, keep_ref, stats_ref, got_ref, got_stats_ref, o0, o1, o2, o3, spread, payload):
    pair, half = place[1], place[2]
    rows_each = keep_ref.shape[1]
    top, total, dots, weights, shifts = merged([[r[n] for n in range(3)] for r in (stats_ref, got_stats_ref)])
    total_hi, dots_hi = total.astype(BF16).astype(F32), dots.astype(BF16).astype(F32)
    tail = jnp.concatenate([top, total_hi, total - total_hi, dots_hi, dots - dots_hi], axis=0)
    spread[...] = jnp.zeros_like(spread)
    for n in range(2):
        spread[n, 8:16, :] = weights[n]
        spread[2 + n, 8:16, :] = weights[n] * shifts[n]
    payload[...] = jnp.zeros_like(payload)
    for b in range(GROUPS):
        w0, w1, c0, c1 = [row_weights(spread.at[n], 2 * b + half, rows_each) for n in range(4)]
        plain0, plain1 = keep_ref[2 * GROUPS + b], got_ref[2 * GROUPS + b].astype(F32)
        payload[b, ATT : ATT + rows_each, :] = w0 * keep_ref[b] + w1 * got_ref[b].astype(F32)
        payload[b, CENTRED : CENTRED + rows_each, :] = (
            w0 * keep_ref[GROUPS + b] + w1 * got_ref[GROUPS + b].astype(F32) - c0 * plain0 - c1 * plain1
        )
        payload[b, PLAIN : PLAIN + rows_each, :] = w0 * plain0 + w1 * plain1
        payload[b, STATS:, :] = tail
    for j, out in enumerate((o0, o1, o2, o3)):
        out[...] = payload[lax.bitwise_xor(pair, j)].astype(BF16)


def read_stats(parts):
    tails = [p[STATS:, :].astype(F32) for p in parts]
    return merged([[t[0:8], t[8:16] + t[16:24], t[24:32] + t[32:40]] for t in tails])


def finish_kernel(place, p0, p1, p2, p3, out_ref, spread):
    rows_each = out_ref.shape[1]
    parts = (p0, p1, p2, p3)
    _, total, _, weights, shifts = read_stats(parts)
    spread[...] = jnp.zeros_like(spread)
    att = jnp.zeros(out_ref.shape[1:], F32)
    grad = jnp.zeros(out_ref.shape[1:], F32)
    for n, part in enumerate(parts):
        spread[0, 8:16, :] = weights[n] / total
        spread[1, 8:16, :] = weights[n] / total * shifts[n]
        w, c = [row_weights(spread.at[m], 2 * place[1] + place[2], rows_each) for m in range(2)]
        rows = part[...].astype(F32)
        att += w * rows[ATT : ATT + rows_each]
        grad += w * rows[CENTRED : CENTRED + rows_each] - c * rows[PLAIN : PLAIN + rows_each]
    out_ref[0] = att.astype(BF16)
    out_ref[1] = (grad * SCALE).astype(BF16)


def backward_kernel(place, ws_ref, q_ref, s0, s1, s2, s3, d_ref, p0, p1, p2, p3, o0, o1, o2, o3, bias, stats):
    kv_len = s0.shape[1]
    slots = (s0, s1, s2, s3)
    set_mask(place, ws_ref, bias)
    top, total, dots, _, _ = read_stats((p0, p1, p2, p3))
    stats[0], stats[1], stats[2] = top, 1.0 / total, dots
    for h in range(GROUP_HEADS):
        kh = joined(slots, 0, head(h))
        vh = joined(slots, 1, head(h))
        qh = q_ref[:, head(h)]
        dh = d_ref[head(h), :]
        scores = mm(kh, qh, NT) * SCALE + bias[...]
        probs = jnp.exp(scores - stats[0, h : h + 1, :]) * stats[1, h : h + 1, :]
        dscores = (probs * (mm(vh, dh, NN) - stats[2, h : h + 1, :])).astype(BF16)
        gk = (mm(dscores, qh, NN) * SCALE).astype(BF16)
        gv = mm(probs.astype(BF16), dh, NT).astype(BF16)
        for s, out in enumerate((o0, o1, o2, o3)):
            part = slice(s * kv_len, (s + 1) * kv_len)
            out[0, :, head(h)] = gk[part]
            out[1, :, head(h)] = gv[part]


def weight_kernel(rows_ref, cot_ref, out_ref, gq_ref, full):
    pieces, _, width = out_ref.shape
    full[...] = mm(rows_ref[0], cot_ref[...], NT)
    gq_ref[...] = rows_ref[1]
    for s in range(pieces):
        x_hi, y = divmod(s, pieces // 2)
        out_ref[2 * y + x_hi] = full[:, s * width : (s + 1) * width].astype(BF16)


def sum_y_kernel(place, x_ref, keep_ref, send_ref):
    x_hi = place[3]
    half = x_ref.shape[0] // 2
    keep_ref[...] = sum(x_ref[2 * y + x_hi].astype(F32) for y in range(half))
    send_ref[...] = sum(x_ref[2 * y + 1 - x_hi].astype(F32) for y in range(half)).astype(BF16)


def sum_kernel(keep_ref, got_ref, out_ref):
    out_ref[...] = (keep_ref[...] + got_ref[...].astype(F32)).astype(BF16)


SMEM = pl.BlockSpec(memory_space=pltpu.SMEM)
ANY = pl.BlockSpec(memory_space=pl.ANY)
WHOLE = pl.BlockSpec(memory_space=pltpu.VMEM)


def call(name, kernel, n_in, out_shapes, scratch=(), scalars=1, in_blocks=None, out_blocks=None, limit=VMEM_LIMIT):
    return pl.pallas_call(
        kernel,
        out_shape=out_shapes,
        in_specs=[SMEM] * scalars + (in_blocks or [WHOLE] * n_in),
        out_specs=out_blocks or jax.tree.map(lambda _: WHOLE, out_shapes),
        scratch_shapes=list(scratch),
        compiler_params=pltpu.CompilerParams(vmem_limit_bytes=limit),
        cost_estimate=pl.CostEstimate(flops=int(COST[name] * 1e9), bytes_accessed=0, transcendentals=0),
        name=name,
    )


def swap_chip(x, s):
    return lax.ppermute(x, ("zl", "x_lo"), [(i, i ^ s) for i in range(GROUPS)])


def swap_pair(x, j):
    return lax.ppermute(x, "zp", [(i, i ^ j) for i in range(GROUPS)])


def swap_half(x):
    return lax.ppermute(x, "core", [(0, 1), (1, 0)])


ALL = [(a, b) for a in range(GROUPS) for b in range(GROUPS)]


def trade(x):
    return lax.ppermute(x, ("zp", "zl", "x_lo"), [(a * GROUPS + b, b * GROUPS + a) for a, b in ALL])


def spread(x, j):
    pairs = [((a * GROUPS + b) * 2 + c, ((b ^ j ^ (2 * c)) * GROUPS + a) * 2 + c) for a, b in ALL for c in range(2)]
    return lax.ppermute(x, SEQ_AXES, pairs)


def local(queries, keys, values, out_grad, w_out, window_start):
    query, key_rows, value_rows, cotangent = queries[0], keys[0], values[0], out_grad[0].T
    q_len = query.shape[0]
    kv_len, width = key_rows.shape
    rows_each, model = w_out.shape
    sections = lax.axis_size(SECTION_AXES)
    place = jnp.stack([lax.axis_index(("zl", "x_lo")), lax.axis_index("zp"), lax.axis_index("core"), lax.axis_index("x_hi")]).astype(jnp.int32)
    starts = window_start.reshape(1, q_len)
    sds = jax.ShapeDtypeStruct
    slots4 = [sds((2, kv_len, GROUP_WIDTH), BF16)] * GROUPS
    bias = pltpu.VMEM((GROUPS * kv_len, q_len), F32)
    features = pltpu.VMEM((GROUP_WIDTH, q_len), F32)
    pieces = pltpu.VMEM((PIECES, rows_each, q_len), F32)

    whole = pltpu.VMEM((kv_len, width), BF16)
    *send, q_own = call(
        "pack",
        pack_kernel,
        3,
        slots4 + [sds((q_len, GROUP_WIDTH), BF16)],
        [whole, whole, pltpu.VMEM((q_len, width), BF16), pltpu.SemaphoreType.DMA((3,))],
        in_blocks=[ANY] * 3,
        limit=60 * 1024 * 1024,
    )(place, key_rows, value_rows, query)
    w_out, send = lax.optimization_barrier((w_out, send))
    slots = [send[0]] + [swap_chip(send[s], s) for s in range(1, GROUPS)]
    d_own = lax.dot_general(w_out, cotangent, NN, preferred_element_type=F32).astype(BF16)
    both = jnp.stack([d_own, swap_half(d_own)])
    mine = [spread(both, j) for j in range(2)]
    theirs = [swap_half(m) for m in mine]
    d_group = call("join", join_kernel, 4, sds((GROUP_WIDTH, q_len), BF16), [pieces, features])(place, *mine, *theirs)

    keep, half, stats = call(
        "forward",
        forward_kernel,
        7,
        [sds((3 * GROUPS, rows_each, q_len), F32), sds((3 * GROUPS, rows_each, q_len), BF16), sds((3, 8, q_len), F32)],
        [bias, features, features, features, pieces],
    )(place, starts, q_own, *slots, d_group)
    parts = call(
        "core",
        core_kernel,
        4,
        [sds((STATS + 40, q_len), BF16)] * GROUPS,
        [pltpu.VMEM((4, 24, q_len), F32), pltpu.VMEM((GROUPS, STATS + 40, q_len), F32)],
    )(place, keep, stats, swap_half(half), swap_half(stats))
    far = swap_pair(parts[2], 2)
    parts = [parts[0], swap_pair(parts[1], 1), far, swap_pair(parts[3], 3)]
    rows = call("finish", finish_kernel, 4, sds((2, rows_each, q_len), BF16), [pltpu.VMEM((2, 24, q_len), F32)])(place, *parts)
    rows, parts = lax.optimization_barrier((rows, parts))
    rows = trade(rows)

    back = call("backward", backward_kernel, 11, slots4, [bias, pltpu.VMEM((3, 8, q_len), F32)])(
        place, starts, q_own, *slots, d_group, *parts
    )
    rows, back = lax.optimization_barrier((rows, back))
    back = [back[0]] + [swap_chip(back[s], s) for s in range(1, GROUPS)]

    part = model // sections
    gw, grad_q = call(
        "weight",
        weight_kernel,
        2,
        [sds((sections, rows_each, part), BF16), sds((rows_each, q_len), BF16)],
        [pltpu.VMEM((rows_each, model), F32)],
        scalars=0,
        limit=SMALL_LIMIT,
    )(rows, cotangent)
    gw = lax.all_to_all(gw, "y", 0, 0, tiled=True)

    def unpack(which, name, back):
        kernel = functools.partial(unpack_kernel, which)
        out = sds((kv_len, width), BF16)
        return call(name, kernel, 4, out, [whole, pltpu.SemaphoreType.DMA], out_blocks=ANY, limit=SMALL_LIMIT)(place, *back)

    grad_k = unpack(0, "unpack_k", back)
    gw, grad_k = lax.optimization_barrier((gw, grad_k))
    keep, half = call("sum_y", sum_y_kernel, 1, [sds((rows_each, part), F32), sds((rows_each, part), BF16)], limit=SMALL_LIMIT)(place, gw)
    keep, back = lax.optimization_barrier((keep, back))
    grad_v = unpack(1, "unpack_v", back)
    half = lax.ppermute(half, "x_hi", [(0, 1), (1, 0)])
    grad_weight = call("sum", sum_kernel, 2, sds((rows_each, part), BF16), scalars=0, limit=SMALL_LIMIT)(keep, half)
    return grad_q[None], grad_k[None], grad_v[None], grad_weight


def solution(mesh):
    fine = Mesh(mesh.devices.reshape(2, mesh.shape["section"] // 2, GROUPS, 2, 2, 2), SECTION_AXES + SEQ_AXES)
    return jax.shard_map(
        local,
        mesh=fine,
        in_specs=(
            P(SECTION_AXES, None, None),
            P(SECTION_AXES, SEQ_AXES, None),
            P(SECTION_AXES, SEQ_AXES, None),
            P(SECTION_AXES, None, None),
            P(SEQ_AXES, None),
            P(),
        ),
        out_specs=(
            P(SECTION_AXES, SEQ_AXES, None),
            P(SECTION_AXES, SEQ_AXES, None),
            P(SECTION_AXES, SEQ_AXES, None),
            P(SEQ_AXES, SECTION_AXES),
        ),
        check_vma=False,
    )
```

```python
import functools

import jax
import jax.numpy as jnp
from jax import lax
from jax.experimental import pallas as pl
from jax.experimental.pallas import tpu as pltpu
from jax.sharding import Mesh, PartitionSpec as P

HEADS = 28
HEAD_DIM = 96
GROUPS = 4
GROUP_HEADS = HEADS // GROUPS
GROUP_WIDTH = GROUP_HEADS * HEAD_DIM
PIECES = 8
NEG = -(2.0**99)
ATT, CENTRED, PLAIN, STATS = 0, 88, 176, 264
SCALE = HEAD_DIM ** (-0.5)
SECTION_AXES = ("x_hi", "y")
SEQ_AXES = ("zp", "zl", "x_lo", "core")
F32 = jnp.float32
BF16 = jnp.bfloat16
VMEM_LIMIT = 32 * 1024 * 1024
SMALL_LIMIT = 16 * 1024 * 1024
COST = dict(
    pack=1, own=1, join=1, forward=2, core=1, finish=1, backward=3, weight=2, unpack_k=10, unpack_v=3, sum_y=0, sum=0
)
NT = (((1,), (1,)), ((), ()))
NN = (((1,), (0,)), ((), ()))
TN = (((0,), (0,)), ((), ()))


def mm(a, b, dims):
    return lax.dot_general(a, b, dims, preferred_element_type=F32)


def pack_kernel(place, k_hbm, v_hbm, o1, o2, o3, k_all, v_all, sems):
    chip = place[0]
    copies = [pltpu.make_async_copy(src, dst, sems.at[n]) for n, (src, dst) in enumerate(((k_hbm, k_all), (v_hbm, v_all)))]
    for copy in copies:
        copy.start()
    for n, (copy, rows) in enumerate(zip(copies, (k_all, v_all))):
        copy.wait()
        for g in range(GROUPS):
            for s, out in enumerate((o1, o2, o3), 1):

                @pl.when(lax.bitwise_xor(chip, s) == g)
                def _():
                    out[n] = rows[:, g * GROUP_WIDTH : (g + 1) * GROUP_WIDTH]


def own_kernel(place, k_ref, v_ref, q_ref, own_ref, q_own_ref):
    for g in range(GROUPS):

        @pl.when(place[0] == g)
        def _():
            cols = slice(g * GROUP_WIDTH, (g + 1) * GROUP_WIDTH)
            own_ref[0] = k_ref[:, cols]
            own_ref[1] = v_ref[:, cols]
            q_own_ref[...] = q_ref[:, cols]


def unpack_kernel(which, place, s0, s1, s2, s3, out_ref, rows, sem):
    chip = place[0]
    for g in range(GROUPS):
        cols = slice(g * GROUP_WIDTH, (g + 1) * GROUP_WIDTH)
        for s, slot in enumerate((s0, s1, s2, s3)):

            @pl.when(lax.bitwise_xor(chip, s) == g)
            def _():
                rows[:, cols] = slot[which]

    copy = pltpu.make_async_copy(rows, out_ref, sem)
    copy.start()
    copy.wait()


def set_mask(place, ws_ref, bias):
    chip, pair, half = place[0], place[1], place[2]
    q_len = ws_ref.shape[1]
    kv_len = bias.shape[0] // GROUPS
    context = kv_len * GROUPS * PIECES
    rows = lax.broadcasted_iota(jnp.int32, (kv_len, q_len), 0)
    query_pos = context - q_len + lax.broadcasted_iota(jnp.int32, (kv_len, q_len), 1)
    for s in range(GROUPS):
        owner = pair * PIECES + 2 * lax.bitwise_xor(chip, s) + half
        key_pos = owner * kv_len + rows
        visible = (key_pos >= ws_ref[...]) & (key_pos <= query_pos)
        bias[s * kv_len : (s + 1) * kv_len, :] = jnp.where(visible, 0.0, NEG)


def join_kernel(place, m0, m1, t0, t1, out_ref, pieces, rows):
    pair, half = place[1], place[2]
    rows_each = m0.shape[1]
    for j, (mine, theirs) in enumerate(((m0, t0), (m1, t1))):
        at = 2 * lax.bitwise_xor(pair, 2 * half + j)
        pieces[at + half] = mine[0].astype(F32)
        pieces[at + 1 - half] = mine[1].astype(F32)
        at = 2 * lax.bitwise_xor(pair, 2 * (1 - half) + j)
        pieces[at + 1 - half] = theirs[0].astype(F32)
        pieces[at + half] = theirs[1].astype(F32)
    for k in range(PIECES):
        rows[k * rows_each : (k + 1) * rows_each, :] = pieces[k]
    out_ref[...] = rows[...].astype(BF16)


def head(h):
    return slice(h * HEAD_DIM, (h + 1) * HEAD_DIM)


def joined(slots, which, cols):
    return jnp.concatenate([s[which, :, cols] for s in slots], axis=0)


def halve(place, full, pieces, at, keep_ref, send_ref):
    half = place[2]
    rows_each = pieces.shape[1]
    for k in range(PIECES):
        pieces[k] = full[k * rows_each : (k + 1) * rows_each, :]
    for b in range(GROUPS):
        keep_ref[at * GROUPS + b] = pieces[2 * b + half]
        send_ref[at * GROUPS + b] = pieces[2 * b + 1 - half].astype(BF16)


def forward_kernel(
    place, ws_ref, q_ref, s0, s1, s2, s3, d_ref, keep_ref, send_ref, stats_ref, bias, att, centred, plain, pieces
):
    slots = (s0, s1, s2, s3)
    set_mask(place, ws_ref, bias)
    stats_ref[...] = jnp.zeros_like(stats_ref)
    for h in range(GROUP_HEADS):
        kh = joined(slots, 0, head(h))
        vh = joined(slots, 1, head(h))
        scores = mm(kh, q_ref[:, head(h)], NT) * SCALE + bias[...]
        top = jnp.floor(jnp.max(scores, axis=0, keepdims=True) * 0.125) * 8.0
        expo = jnp.exp(scores - top)
        total = jnp.sum(expo, axis=0, keepdims=True)
        dprobs = mm(vh, d_ref[head(h), :], NN)
        dots = jnp.sum(expo * dprobs, axis=0, keepdims=True) / total
        expo_b = expo.astype(BF16)
        att[head(h), :] = mm(vh, expo_b, TN)
        plain[head(h), :] = mm(kh, expo_b, TN)
        centred[head(h), :] = mm(kh, (expo * (dprobs - dots)).astype(BF16), TN)
        stats_ref[0, h : h + 1, :] = top
        stats_ref[1, h : h + 1, :] = total
        stats_ref[2, h : h + 1, :] = dots
    for at, full in enumerate((att, centred, plain)):
        halve(place, full, pieces, at, keep_ref, send_ref)


def row_weights(spread, piece, rows_each):
    q_len = spread.shape[1]
    row = lax.broadcasted_iota(jnp.int32, (rows_each, q_len), 0)
    before = spread[pl.ds(piece + 7, 1), :]
    after = spread[pl.ds(piece + 8, 1), :]
    return jnp.where(row < (HEAD_DIM - rows_each) * piece, before, after)


def merged(stats):
    top = functools.reduce(jnp.maximum, [s[0] for s in stats])
    weights = [jnp.exp(s[0] - top) for s in stats]
    total = sum(w * s[1] for w, s in zip(weights, stats))
    total = jnp.where(total > 0.0, total, 1.0)
    dots = sum(w * s[1] * s[2] for w, s in zip(weights, stats)) / total
    return top, total, dots, weights, [dots - s[2] for s in stats]


def core_kernel(place, keep_ref, stats_ref, got_ref, got_stats_ref, o0, o1, o2, o3, spread, payload):
    pair, half = place[1], place[2]
    rows_each = keep_ref.shape[1]
    top, total, dots, weights, shifts = merged([[r[n] for n in range(3)] for r in (stats_ref, got_stats_ref)])
    total_hi, dots_hi = total.astype(BF16).astype(F32), dots.astype(BF16).astype(F32)
    tail = jnp.concatenate([top, total_hi, total - total_hi, dots_hi, dots - dots_hi], axis=0)
    spread[...] = jnp.zeros_like(spread)
    for n in range(2):
        spread[n, 8:16, :] = weights[n]
        spread[2 + n, 8:16, :] = weights[n] * shifts[n]
    payload[...] = jnp.zeros_like(payload)
    for b in range(GROUPS):
        w0, w1, c0, c1 = [row_weights(spread.at[n], 2 * b + half, rows_each) for n in range(4)]
        plain0, plain1 = keep_ref[2 * GROUPS + b], got_ref[2 * GROUPS + b].astype(F32)
        payload[b, ATT : ATT + rows_each, :] = w0 * keep_ref[b] + w1 * got_ref[b].astype(F32)
        payload[b, CENTRED : CENTRED + rows_each, :] = (
            w0 * keep_ref[GROUPS + b] + w1 * got_ref[GROUPS + b].astype(F32) - c0 * plain0 - c1 * plain1
        )
        payload[b, PLAIN : PLAIN + rows_each, :] = w0 * plain0 + w1 * plain1
        payload[b, STATS:, :] = tail
    for j, out in enumerate((o0, o1, o2, o3)):
        out[...] = payload[lax.bitwise_xor(pair, j)].astype(BF16)


def read_stats(parts):
    tails = [p[STATS:, :].astype(F32) for p in parts]
    return merged([[t[0:8], t[8:16] + t[16:24], t[24:32] + t[32:40]] for t in tails])


def finish_kernel(place, p0, p1, p2, p3, out_ref, spread):
    rows_each = out_ref.shape[1]
    parts = (p0, p1, p2, p3)
    _, total, _, weights, shifts = read_stats(parts)
    spread[...] = jnp.zeros_like(spread)
    att = jnp.zeros(out_ref.shape[1:], F32)
    grad = jnp.zeros(out_ref.shape[1:], F32)
    for n, part in enumerate(parts):
        spread[0, 8:16, :] = weights[n] / total
        spread[1, 8:16, :] = weights[n] / total * shifts[n]
        w, c = [row_weights(spread.at[m], 2 * place[1] + place[2], rows_each) for m in range(2)]
        rows = part[...].astype(F32)
        att += w * rows[ATT : ATT + rows_each]
        grad += w * rows[CENTRED : CENTRED + rows_each] - c * rows[PLAIN : PLAIN + rows_each]
    out_ref[0] = att.astype(BF16)
    out_ref[1] = (grad * SCALE).astype(BF16)


def backward_kernel(place, ws_ref, q_ref, s0, s1, s2, s3, d_ref, p0, p1, p2, p3, o0, o1, o2, o3, bias, stats):
    kv_len = s0.shape[1]
    slots = (s0, s1, s2, s3)
    set_mask(place, ws_ref, bias)
    top, total, dots, _, _ = read_stats((p0, p1, p2, p3))
    stats[0], stats[1], stats[2] = top, 1.0 / total, dots
    for h in range(GROUP_HEADS):
        kh = joined(slots, 0, head(h))
        vh = joined(slots, 1, head(h))
        qh = q_ref[:, head(h)]
        dh = d_ref[head(h), :]
        scores = mm(kh, qh, NT) * SCALE + bias[...]
        probs = jnp.exp(scores - stats[0, h : h + 1, :]) * stats[1, h : h + 1, :]
        dscores = (probs * (mm(vh, dh, NN) - stats[2, h : h + 1, :])).astype(BF16)
        gk = (mm(dscores, qh, NN) * SCALE).astype(BF16)
        gv = mm(probs.astype(BF16), dh, NT).astype(BF16)
        for s, out in enumerate((o0, o1, o2, o3)):
            part = slice(s * kv_len, (s + 1) * kv_len)
            out[0, :, head(h)] = gk[part]
            out[1, :, head(h)] = gv[part]


def weight_kernel(rows_ref, cot_ref, out_ref, gq_ref, full):
    pieces, _, width = out_ref.shape
    full[...] = mm(rows_ref[0], cot_ref[...], NT)
    gq_ref[...] = rows_ref[1]
    for s in range(pieces):
        x_hi, y = divmod(s, pieces // 2)
        out_ref[2 * y + x_hi] = full[:, s * width : (s + 1) * width].astype(BF16)


def sum_y_kernel(place, x_ref, keep_ref, send_ref):
    x_hi = place[3]
    half = x_ref.shape[0] // 2
    keep_ref[...] = sum(x_ref[2 * y + x_hi].astype(F32) for y in range(half))
    send_ref[...] = sum(x_ref[2 * y + 1 - x_hi].astype(F32) for y in range(half)).astype(BF16)


def sum_kernel(keep_ref, got_ref, out_ref):
    out_ref[...] = (keep_ref[...] + got_ref[...].astype(F32)).astype(BF16)


SMEM = pl.BlockSpec(memory_space=pltpu.SMEM)
ANY = pl.BlockSpec(memory_space=pl.ANY)
WHOLE = pl.BlockSpec(memory_space=pltpu.VMEM)


def call(name, kernel, n_in, out_shapes, scratch=(), scalars=1, in_blocks=None, out_blocks=None, limit=VMEM_LIMIT):
    return pl.pallas_call(
        kernel,
        out_shape=out_shapes,
        in_specs=[SMEM] * scalars + (in_blocks or [WHOLE] * n_in),
        out_specs=out_blocks or jax.tree.map(lambda _: WHOLE, out_shapes),
        scratch_shapes=list(scratch),
        compiler_params=pltpu.CompilerParams(vmem_limit_bytes=limit),
        cost_estimate=pl.CostEstimate(flops=int(COST[name] * 1e9), bytes_accessed=0, transcendentals=0),
        name=name,
    )


def swap_chip(x, s):
    return lax.ppermute(x, ("zl", "x_lo"), [(i, i ^ s) for i in range(GROUPS)])


def swap_pair(x, j):
    return lax.ppermute(x, "zp", [(i, i ^ j) for i in range(GROUPS)])


def swap_half(x):
    return lax.ppermute(x, "core", [(0, 1), (1, 0)])


ALL = [(a, b) for a in range(GROUPS) for b in range(GROUPS)]


def trade(x):
    return lax.ppermute(x, ("zp", "zl", "x_lo"), [(a * GROUPS + b, b * GROUPS + a) for a, b in ALL])


def spread(x, j):
    pairs = [((a * GROUPS + b) * 2 + c, ((b ^ j ^ (2 * c)) * GROUPS + a) * 2 + c) for a, b in ALL for c in range(2)]
    return lax.ppermute(x, SEQ_AXES, pairs)


def local(queries, keys, values, out_grad, w_out, window_start):
    query, key_rows, value_rows, cotangent = queries[0], keys[0], values[0], out_grad[0].T
    q_len = query.shape[0]
    kv_len, width = key_rows.shape
    rows_each, model = w_out.shape
    sections = lax.axis_size(SECTION_AXES)
    place = jnp.stack([lax.axis_index(("zl", "x_lo")), lax.axis_index("zp"), lax.axis_index("core"), lax.axis_index("x_hi")]).astype(jnp.int32)
    starts = window_start.reshape(1, q_len)
    sds = jax.ShapeDtypeStruct
    slots4 = [sds((2, kv_len, GROUP_WIDTH), BF16)] * GROUPS
    bias = pltpu.VMEM((GROUPS * kv_len, q_len), F32)
    features = pltpu.VMEM((GROUP_WIDTH, q_len), F32)
    pieces = pltpu.VMEM((PIECES, rows_each, q_len), F32)

    whole = pltpu.VMEM((kv_len, width), BF16)
    send = call(
        "pack",
        pack_kernel,
        2,
        slots4[1:],
        [whole, whole, pltpu.SemaphoreType.DMA((2,))],
        in_blocks=[ANY] * 2,
        limit=60 * 1024 * 1024,
    )(place, key_rows, value_rows)
    own, q_own = call("own", own_kernel, 3, [slots4[0], sds((q_len, GROUP_WIDTH), BF16)], limit=SMALL_LIMIT)(
        place, key_rows, value_rows, query
    )
    w_out, send = lax.optimization_barrier((w_out, send))
    slots = [own] + [swap_chip(send[s - 1], s) for s in range(1, GROUPS)]
    d_own = lax.dot_general(w_out, cotangent, NN, preferred_element_type=F32).astype(BF16)
    both = jnp.stack([d_own, swap_half(d_own)])
    mine = [spread(both, j) for j in range(2)]
    theirs = [swap_half(m) for m in mine]
    d_group = call("join", join_kernel, 4, sds((GROUP_WIDTH, q_len), BF16), [pieces, features])(place, *mine, *theirs)

    keep, half, stats = call(
        "forward",
        forward_kernel,
        7,
        [sds((3 * GROUPS, rows_each, q_len), F32), sds((3 * GROUPS, rows_each, q_len), BF16), sds((3, 8, q_len), F32)],
        [bias, features, features, features, pieces],
    )(place, starts, q_own, *slots, d_group)
    parts = call(
        "core",
        core_kernel,
        4,
        [sds((STATS + 40, q_len), BF16)] * GROUPS,
        [pltpu.VMEM((4, 24, q_len), F32), pltpu.VMEM((GROUPS, STATS + 40, q_len), F32)],
    )(place, keep, stats, swap_half(half), swap_half(stats))
    far = swap_pair(parts[2], 2)
    parts = [parts[0], swap_pair(parts[1], 1), far, swap_pair(parts[3], 3)]
    rows = call("finish", finish_kernel, 4, sds((2, rows_each, q_len), BF16), [pltpu.VMEM((2, 24, q_len), F32)])(place, *parts)
    rows, parts = lax.optimization_barrier((rows, parts))
    rows = trade(rows)

    back = call("backward", backward_kernel, 11, slots4, [bias, pltpu.VMEM((3, 8, q_len), F32)])(
        place, starts, q_own, *slots, d_group, *parts
    )
    rows, back = lax.optimization_barrier((rows, back))
    back = [back[0]] + [swap_chip(back[s], s) for s in range(1, GROUPS)]

    part = model // sections
    gw, grad_q = call(
        "weight",
        weight_kernel,
        2,
        [sds((sections, rows_each, part), BF16), sds((rows_each, q_len), BF16)],
        [pltpu.VMEM((rows_each, model), F32)],
        scalars=0,
        limit=SMALL_LIMIT,
    )(rows, cotangent)
    gw = lax.all_to_all(gw, "y", 0, 0, tiled=True)

    def unpack(which, name, back):
        kernel = functools.partial(unpack_kernel, which)
        out = sds((kv_len, width), BF16)
        return call(name, kernel, 4, out, [whole, pltpu.SemaphoreType.DMA], out_blocks=ANY, limit=SMALL_LIMIT)(place, *back)

    grad_k = unpack(0, "unpack_k", back)
    gw, grad_k = lax.optimization_barrier((gw, grad_k))
    keep, half = call("sum_y", sum_y_kernel, 1, [sds((rows_each, part), F32), sds((rows_each, part), BF16)], limit=SMALL_LIMIT)(place, gw)
    keep, back = lax.optimization_barrier((keep, back))
    grad_v = unpack(1, "unpack_v", back)
    half = lax.ppermute(half, "x_hi", [(0, 1), (1, 0)])
    grad_weight = call("sum", sum_kernel, 2, sds((rows_each, part), BF16), scalars=0, limit=SMALL_LIMIT)(keep, half)
    return grad_q[None], grad_k[None], grad_v[None], grad_weight


def solution(mesh):
    fine = Mesh(mesh.devices.reshape(2, mesh.shape["section"] // 2, GROUPS, 2, 2, 2), SECTION_AXES + SEQ_AXES)
    return jax.shard_map(
        local,
        mesh=fine,
        in_specs=(
            P(SECTION_AXES, None, None),
            P(SECTION_AXES, SEQ_AXES, None),
            P(SECTION_AXES, SEQ_AXES, None),
            P(SECTION_AXES, None, None),
            P(SEQ_AXES, None),
            P(),
        ),
        out_specs=(
            P(SECTION_AXES, SEQ_AXES, None),
            P(SECTION_AXES, SEQ_AXES, None),
            P(SECTION_AXES, SEQ_AXES, None),
            P(SEQ_AXES, SECTION_AXES),
        ),
        check_vma=False,
    )
```

```python
import functools

import jax
import jax.numpy as jnp
from jax import lax
from jax.experimental import pallas as pl
from jax.experimental.pallas import tpu as pltpu
from jax.sharding import Mesh, PartitionSpec as P

HEADS = 28
HEAD_DIM = 96
GROUPS = 4
GROUP_HEADS = HEADS // GROUPS
GROUP_WIDTH = GROUP_HEADS * HEAD_DIM
PIECES = 8
NEG = -(2.0**99)
ATT, CENTRED, PLAIN, STATS = 0, 88, 176, 264
SCALE = HEAD_DIM ** (-0.5)
SECTION_AXES = ("x_hi", "y")
SEQ_AXES = ("zp", "zl", "x_lo", "core")
F32 = jnp.float32
BF16 = jnp.bfloat16
VMEM_LIMIT = 32 * 1024 * 1024
SMALL_LIMIT = 16 * 1024 * 1024
COST = dict(
    pack=1, own=1, join=1, forward=2, core=1, finish=1, backward=3, weight=2, unpack_k=10, unpack_v=3, sum_y=0, sum=0
)
NT = (((1,), (1,)), ((), ()))
NN = (((1,), (0,)), ((), ()))
TN = (((0,), (0,)), ((), ()))


def mm(a, b, dims):
    return lax.dot_general(a, b, dims, preferred_element_type=F32)


def pack_kernel(k_hbm, v_hbm, o1, o2, o3, k_all, v_all, sems):
    chip = 2 * lax.axis_index("zl") + lax.axis_index("x_lo")
    copies = [pltpu.make_async_copy(src, dst, sems.at[n]) for n, (src, dst) in enumerate(((k_hbm, k_all), (v_hbm, v_all)))]
    for copy in copies:
        copy.start()
    for n, (copy, rows) in enumerate(zip(copies, (k_all, v_all))):
        copy.wait()
        for g in range(GROUPS):
            for s, out in enumerate((o1, o2, o3), 1):

                @pl.when(lax.bitwise_xor(chip, s) == g)
                def _():
                    out[n] = rows[:, g * GROUP_WIDTH : (g + 1) * GROUP_WIDTH]


def own_kernel(place, k_ref, v_ref, q_ref, own_ref, q_own_ref):
    for g in range(GROUPS):

        @pl.when(place[0] == g)
        def _():
            cols = slice(g * GROUP_WIDTH, (g + 1) * GROUP_WIDTH)
            own_ref[0] = k_ref[:, cols]
            own_ref[1] = v_ref[:, cols]
            q_own_ref[...] = q_ref[:, cols]


def unpack_kernel(which, place, s0, s1, s2, s3, out_ref, parts, rows, sems):
    chip = place[0]
    slots = (s0, s1, s2, s3)
    copies = [pltpu.make_async_copy(slot.at[which], parts.at[s], sems.at[s]) for s, slot in enumerate(slots)]
    for copy in copies:
        copy.start()
    for s, copy in enumerate(copies):
        copy.wait()
        for g in range(GROUPS):

            @pl.when(lax.bitwise_xor(chip, s) == g)
            def _():
                rows[:, g * GROUP_WIDTH : (g + 1) * GROUP_WIDTH] = parts[s]

    copy = pltpu.make_async_copy(rows, out_ref, sems.at[GROUPS])
    copy.start()
    copy.wait()


def set_mask(place, ws_ref, bias):
    chip, pair, half = place[0], place[1], place[2]
    q_len = ws_ref.shape[1]
    kv_len = bias.shape[0] // GROUPS
    context = kv_len * GROUPS * PIECES
    rows = lax.broadcasted_iota(jnp.int32, (kv_len, q_len), 0)
    query_pos = context - q_len + lax.broadcasted_iota(jnp.int32, (kv_len, q_len), 1)
    for s in range(GROUPS):
        owner = pair * PIECES + 2 * lax.bitwise_xor(chip, s) + half
        key_pos = owner * kv_len + rows
        visible = (key_pos >= ws_ref[...]) & (key_pos <= query_pos)
        bias[s * kv_len : (s + 1) * kv_len, :] = jnp.where(visible, 0.0, NEG)


def join_kernel(place, m0, m1, t0, t1, out_ref, pieces, rows):
    pair, half = place[1], place[2]
    rows_each = m0.shape[1]
    for j, (mine, theirs) in enumerate(((m0, t0), (m1, t1))):
        at = 2 * lax.bitwise_xor(pair, 2 * half + j)
        pieces[at + half] = mine[0].astype(F32)
        pieces[at + 1 - half] = mine[1].astype(F32)
        at = 2 * lax.bitwise_xor(pair, 2 * (1 - half) + j)
        pieces[at + 1 - half] = theirs[0].astype(F32)
        pieces[at + half] = theirs[1].astype(F32)
    for k in range(PIECES):
        rows[k * rows_each : (k + 1) * rows_each, :] = pieces[k]
    out_ref[...] = rows[...].astype(BF16)


def head(h):
    return slice(h * HEAD_DIM, (h + 1) * HEAD_DIM)


def joined(slots, which, cols):
    return jnp.concatenate([s[which, :, cols] for s in slots], axis=0)


def halve(place, full, pieces, at, keep_ref, send_ref):
    half = place[2]
    rows_each = pieces.shape[1]
    for k in range(PIECES):
        pieces[k] = full[k * rows_each : (k + 1) * rows_each, :]
    for b in range(GROUPS):
        keep_ref[at * GROUPS + b] = pieces[2 * b + half]
        send_ref[at * GROUPS + b] = pieces[2 * b + 1 - half].astype(BF16)


def forward_kernel(
    place, ws_ref, q_ref, s0, s1, s2, s3, d_ref, keep_ref, send_ref, stats_ref, bias, att, centred, plain, pieces
):
    slots = (s0, s1, s2, s3)
    set_mask(place, ws_ref, bias)
    stats_ref[...] = jnp.zeros_like(stats_ref)
    for h in range(GROUP_HEADS):
        kh = joined(slots, 0, head(h))
        vh = joined(slots, 1, head(h))
        scores = mm(kh, q_ref[:, head(h)], NT) * SCALE + bias[...]
        top = jnp.floor(jnp.max(scores, axis=0, keepdims=True) * 0.125) * 8.0
        expo = jnp.exp(scores - top)
        total = jnp.sum(expo, axis=0, keepdims=True)
        dprobs = mm(vh, d_ref[head(h), :], NN)
        dots = jnp.sum(expo * dprobs, axis=0, keepdims=True) / total
        expo_b = expo.astype(BF16)
        att[head(h), :] = mm(vh, expo_b, TN)
        plain[head(h), :] = mm(kh, expo_b, TN)
        centred[head(h), :] = mm(kh, (expo * (dprobs - dots)).astype(BF16), TN)
        stats_ref[0, h : h + 1, :] = top
        stats_ref[1, h : h + 1, :] = total
        stats_ref[2, h : h + 1, :] = dots
    for at, full in enumerate((att, centred, plain)):
        halve(place, full, pieces, at, keep_ref, send_ref)


def row_weights(spread, piece, rows_each):
    q_len = spread.shape[1]
    row = lax.broadcasted_iota(jnp.int32, (rows_each, q_len), 0)
    before = spread[pl.ds(piece + 7, 1), :]
    after = spread[pl.ds(piece + 8, 1), :]
    return jnp.where(row < (HEAD_DIM - rows_each) * piece, before, after)


def merged(stats):
    top = functools.reduce(jnp.maximum, [s[0] for s in stats])
    weights = [jnp.exp(s[0] - top) for s in stats]
    total = sum(w * s[1] for w, s in zip(weights, stats))
    total = jnp.where(total > 0.0, total, 1.0)
    dots = sum(w * s[1] * s[2] for w, s in zip(weights, stats)) / total
    return top, total, dots, weights, [dots - s[2] for s in stats]


def core_kernel(place, keep_ref, stats_ref, got_ref, got_stats_ref, o0, o1, o2, o3, spread, payload):
    pair, half = place[1], place[2]
    rows_each = keep_ref.shape[1]
    top, total, dots, weights, shifts = merged([[r[n] for n in range(3)] for r in (stats_ref, got_stats_ref)])
    total_hi, dots_hi = total.astype(BF16).astype(F32), dots.astype(BF16).astype(F32)
    tail = jnp.concatenate([top, total_hi, total - total_hi, dots_hi, dots - dots_hi], axis=0)
    spread[...] = jnp.zeros_like(spread)
    for n in range(2):
        spread[n, 8:16, :] = weights[n]
        spread[2 + n, 8:16, :] = weights[n] * shifts[n]
    payload[...] = jnp.zeros_like(payload)
    for b in range(GROUPS):
        w0, w1, c0, c1 = [row_weights(spread.at[n], 2 * b + half, rows_each) for n in range(4)]
        plain0, plain1 = keep_ref[2 * GROUPS + b], got_ref[2 * GROUPS + b].astype(F32)
        payload[b, ATT : ATT + rows_each, :] = w0 * keep_ref[b] + w1 * got_ref[b].astype(F32)
        payload[b, CENTRED : CENTRED + rows_each, :] = (
            w0 * keep_ref[GROUPS + b] + w1 * got_ref[GROUPS + b].astype(F32) - c0 * plain0 - c1 * plain1
        )
        payload[b, PLAIN : PLAIN + rows_each, :] = w0 * plain0 + w1 * plain1
        payload[b, STATS:, :] = tail
    for j, out in enumerate((o0, o1, o2, o3)):
        out[...] = payload[lax.bitwise_xor(pair, j)].astype(BF16)


def read_stats(parts):
    tails = [p[STATS:, :].astype(F32) for p in parts]
    return merged([[t[0:8], t[8:16] + t[16:24], t[24:32] + t[32:40]] for t in tails])


def finish_kernel(place, p0, p1, p2, p3, out_ref, spread):
    rows_each = out_ref.shape[1]
    parts = (p0, p1, p2, p3)
    _, total, _, weights, shifts = read_stats(parts)
    spread[...] = jnp.zeros_like(spread)
    att = jnp.zeros(out_ref.shape[1:], F32)
    grad = jnp.zeros(out_ref.shape[1:], F32)
    for n, part in enumerate(parts):
        spread[0, 8:16, :] = weights[n] / total
        spread[1, 8:16, :] = weights[n] / total * shifts[n]
        w, c = [row_weights(spread.at[m], 2 * place[1] + place[2], rows_each) for m in range(2)]
        rows = part[...].astype(F32)
        att += w * rows[ATT : ATT + rows_each]
        grad += w * rows[CENTRED : CENTRED + rows_each] - c * rows[PLAIN : PLAIN + rows_each]
    out_ref[0] = att.astype(BF16)
    out_ref[1] = (grad * SCALE).astype(BF16)


def backward_kernel(place, ws_ref, q_ref, s0, s1, s2, s3, d_ref, p0, p1, p2, p3, o0, o1, o2, o3, bias, stats):
    kv_len = s0.shape[1]
    slots = (s0, s1, s2, s3)
    set_mask(place, ws_ref, bias)
    top, total, dots, _, _ = read_stats((p0, p1, p2, p3))
    stats[0], stats[1], stats[2] = top, 1.0 / total, dots
    for h in range(GROUP_HEADS):
        kh = joined(slots, 0, head(h))
        vh = joined(slots, 1, head(h))
        qh = q_ref[:, head(h)]
        dh = d_ref[head(h), :]
        scores = mm(kh, qh, NT) * SCALE + bias[...]
        probs = jnp.exp(scores - stats[0, h : h + 1, :]) * stats[1, h : h + 1, :]
        dscores = (probs * (mm(vh, dh, NN) - stats[2, h : h + 1, :])).astype(BF16)
        gk = (mm(dscores, qh, NN) * SCALE).astype(BF16)
        gv = mm(probs.astype(BF16), dh, NT).astype(BF16)
        for s, out in enumerate((o0, o1, o2, o3)):
            part = slice(s * kv_len, (s + 1) * kv_len)
            out[0, :, head(h)] = gk[part]
            out[1, :, head(h)] = gv[part]


def weight_kernel(rows_ref, cot_ref, out_ref, gq_ref, full):
    pieces, _, width = out_ref.shape
    full[...] = mm(rows_ref[0], cot_ref[...], NT)
    gq_ref[...] = rows_ref[1]
    for s in range(pieces):
        x_hi, y = divmod(s, pieces // 2)
        out_ref[2 * y + x_hi] = full[:, s * width : (s + 1) * width].astype(BF16)


def sum_y_kernel(place, x_ref, keep_ref, send_ref):
    x_hi = place[3]
    half = x_ref.shape[0] // 2
    keep_ref[...] = sum(x_ref[2 * y + x_hi].astype(F32) for y in range(half))
    send_ref[...] = sum(x_ref[2 * y + 1 - x_hi].astype(F32) for y in range(half)).astype(BF16)


def sum_kernel(keep_ref, got_ref, out_ref):
    out_ref[...] = (keep_ref[...] + got_ref[...].astype(F32)).astype(BF16)


SMEM = pl.BlockSpec(memory_space=pltpu.SMEM)
ANY = pl.BlockSpec(memory_space=pl.ANY)
WHOLE = pl.BlockSpec(memory_space=pltpu.VMEM)


def call(name, kernel, n_in, out_shapes, scratch=(), scalars=1, in_blocks=None, out_blocks=None, limit=VMEM_LIMIT):
    return pl.pallas_call(
        kernel,
        out_shape=out_shapes,
        in_specs=[SMEM] * scalars + (in_blocks or [WHOLE] * n_in),
        out_specs=out_blocks or jax.tree.map(lambda _: WHOLE, out_shapes),
        scratch_shapes=list(scratch),
        compiler_params=pltpu.CompilerParams(vmem_limit_bytes=limit),
        cost_estimate=pl.CostEstimate(flops=int(COST[name] * 1e9), bytes_accessed=0, transcendentals=0),
        name=name,
    )


def swap_chip(x, s):
    return lax.ppermute(x, ("zl", "x_lo"), [(i, i ^ s) for i in range(GROUPS)])


def swap_pair(x, j):
    return lax.ppermute(x, "zp", [(i, i ^ j) for i in range(GROUPS)])


def swap_half(x):
    return lax.ppermute(x, "core", [(0, 1), (1, 0)])


ALL = [(a, b) for a in range(GROUPS) for b in range(GROUPS)]


def trade(x):
    return lax.ppermute(x, ("zp", "zl", "x_lo"), [(a * GROUPS + b, b * GROUPS + a) for a, b in ALL])


def spread(x, j):
    pairs = [((a * GROUPS + b) * 2 + c, ((b ^ j ^ (2 * c)) * GROUPS + a) * 2 + c) for a, b in ALL for c in range(2)]
    return lax.ppermute(x, SEQ_AXES, pairs)


def local(queries, keys, values, out_grad, w_out, window_start):
    query, key_rows, value_rows, cotangent = queries[0], keys[0], values[0], out_grad[0].T
    q_len = query.shape[0]
    kv_len, width = key_rows.shape
    rows_each, model = w_out.shape
    sections = lax.axis_size(SECTION_AXES)
    place = jnp.stack([lax.axis_index(("zl", "x_lo")), lax.axis_index("zp"), lax.axis_index("core"), lax.axis_index("x_hi")]).astype(jnp.int32)
    starts = window_start.reshape(1, q_len)
    sds = jax.ShapeDtypeStruct
    slots4 = [sds((2, kv_len, GROUP_WIDTH), BF16)] * GROUPS
    bias = pltpu.VMEM((GROUPS * kv_len, q_len), F32)
    features = pltpu.VMEM((GROUP_WIDTH, q_len), F32)
    pieces = pltpu.VMEM((PIECES, rows_each, q_len), F32)

    whole = pltpu.VMEM((kv_len, width), BF16)
    send = call(
        "pack",
        pack_kernel,
        2,
        slots4[1:],
        [whole, whole, pltpu.SemaphoreType.DMA((2,))],
        in_blocks=[ANY] * 2,
        scalars=0,
        limit=60 * 1024 * 1024,
    )(key_rows, value_rows)
    own, q_own = call("own", own_kernel, 3, [slots4[0], sds((q_len, GROUP_WIDTH), BF16)], limit=SMALL_LIMIT)(
        place, key_rows, value_rows, query
    )
    w_out, send = lax.optimization_barrier((w_out, send))
    slots = [own] + [swap_chip(send[s - 1], s) for s in range(1, GROUPS)]
    d_own = lax.dot_general(w_out, cotangent, NN, preferred_element_type=F32).astype(BF16)
    both = jnp.stack([d_own, swap_half(d_own)])
    mine = [spread(both, j) for j in range(2)]
    theirs = [swap_half(m) for m in mine]
    d_group = call("join", join_kernel, 4, sds((GROUP_WIDTH, q_len), BF16), [pieces, features])(place, *mine, *theirs)

    keep, half, stats = call(
        "forward",
        forward_kernel,
        7,
        [sds((3 * GROUPS, rows_each, q_len), F32), sds((3 * GROUPS, rows_each, q_len), BF16), sds((3, 8, q_len), F32)],
        [bias, features, features, features, pieces],
    )(place, starts, q_own, *slots, d_group)
    parts = call(
        "core",
        core_kernel,
        4,
        [sds((STATS + 40, q_len), BF16)] * GROUPS,
        [pltpu.VMEM((4, 24, q_len), F32), pltpu.VMEM((GROUPS, STATS + 40, q_len), F32)],
    )(place, keep, stats, swap_half(half), swap_half(stats))
    far = swap_pair(parts[2], 2)
    parts = [parts[0], swap_pair(parts[1], 1), far, swap_pair(parts[3], 3)]
    rows = call("finish", finish_kernel, 4, sds((2, rows_each, q_len), BF16), [pltpu.VMEM((2, 24, q_len), F32)])(place, *parts)
    rows, parts = lax.optimization_barrier((rows, parts))
    rows = trade(rows)

    back = call("backward", backward_kernel, 11, slots4, [bias, pltpu.VMEM((3, 8, q_len), F32)])(
        place, starts, q_own, *slots, d_group, *parts
    )
    rows, back = lax.optimization_barrier((rows, back))
    back = [back[0]] + [swap_chip(back[s], s) for s in range(1, GROUPS)]

    part = model // sections
    gw, grad_q = call(
        "weight",
        weight_kernel,
        2,
        [sds((sections, rows_each, part), BF16), sds((rows_each, q_len), BF16)],
        [pltpu.VMEM((rows_each, model), F32)],
        scalars=0,
        limit=SMALL_LIMIT,
    )(rows, cotangent)
    gw = lax.all_to_all(gw, "y", 0, 0, tiled=True)

    def unpack(which, name, back):
        kernel = functools.partial(unpack_kernel, which)
        out = sds((kv_len, width), BF16)
        scratch = [pltpu.VMEM((GROUPS, kv_len, GROUP_WIDTH), BF16), whole, pltpu.SemaphoreType.DMA((GROUPS + 1,))]
        return call(name, kernel, 4, out, scratch, in_blocks=[ANY] * 4, out_blocks=ANY, limit=SMALL_LIMIT)(place, *back)

    grad_k = unpack(0, "unpack_k", back)
    gw, grad_k = lax.optimization_barrier((gw, grad_k))
    keep, half = call("sum_y", sum_y_kernel, 1, [sds((rows_each, part), F32), sds((rows_each, part), BF16)], limit=SMALL_LIMIT)(place, gw)
    keep, back = lax.optimization_barrier((keep, back))
    grad_v = unpack(1, "unpack_v", back)
    half = lax.ppermute(half, "x_hi", [(0, 1), (1, 0)])
    grad_weight = call("sum", sum_kernel, 2, sds((rows_each, part), BF16), scalars=0, limit=SMALL_LIMIT)(keep, half)
    return grad_q[None], grad_k[None], grad_v[None], grad_weight


def solution(mesh):
    fine = Mesh(mesh.devices.reshape(2, mesh.shape["section"] // 2, GROUPS, 2, 2, 2), SECTION_AXES + SEQ_AXES)
    return jax.shard_map(
        local,
        mesh=fine,
        in_specs=(
            P(SECTION_AXES, None, None),
            P(SECTION_AXES, SEQ_AXES, None),
            P(SECTION_AXES, SEQ_AXES, None),
            P(SECTION_AXES, None, None),
            P(SEQ_AXES, None),
            P(),
        ),
        out_specs=(
            P(SECTION_AXES, SEQ_AXES, None),
            P(SECTION_AXES, SEQ_AXES, None),
            P(SECTION_AXES, SEQ_AXES, None),
            P(SEQ_AXES, SECTION_AXES),
        ),
        check_vma=False,
    )
```
